128 devices in a mesh: row: 4 (over y), col: 32 (over z, x, core).
Axes of the slice: x: 4, y: 4, z: 4, core: 2. Of those that a mesh axis runs over, the one named last changes fastest.
Arguments:
- row_points: bfloat16 [98304, 64], P(('row', 'col')), as said below
- col_points: bfloat16 [32768, 64], P('col'), as said below
- row_logmass: bfloat16 [98304], P(('row', 'col')), may hold values from -4 to 4
- col_logmass: float32 [32768], P('col'), may hold values from -4 to 4
- col_potential: float32 [32768], P('col'), may hold values from -3 to 11
Outputs:
- row_potential: float32 [98304], P('row')
- new_col_potential: float32 [32768], P('col')
The draws below stay inside these ranges and needn't reach their ends.
Inputs may be any that keep to these rules, and one draw needn't show every extreme that they name: `row_points`: latent coordinates. `col_points`: latent coordinates.
All inputs are finite; a program needn't handle non-finite values.
Results may differ from the reference program's by a relative error of at most 0.0008.
Values may be sent and summed in bfloat16 or wider, within the bound.
No kernel may reach another device: no remote copies, remote signals or barrier semaphores. Data moves between devices by JAX's collectives and lax.ppermute only.
A program may use at most 64 MiB of HBM per device.

```python
import jax
import jax.numpy as jnp
from jax import lax

DIM = 64
N = 98304
M = 32768


def column_cloud(key):
    first = jax.random.normal(jax.random.fold_in(key, 11), (M, DIM), jnp.float32)
    mixed = jnp.clip(first, -6.0, 6.0)
    return 0.3 * mixed


def draw_col_points(key, part):
    cloud = column_cloud(key)
    return cloud.astype(jnp.bfloat16)


def draw_row_points(key, part):
    key = jax.random.fold_in(key, 3)
    key_own = jax.random.fold_in(key, 0)
    points = 0.3 * jnp.clip(jax.random.normal(key_own, (N, DIM), jnp.float32), -6.0, 6.0)
    return points.astype(jnp.bfloat16)


def draw_col_potential(key, part):
    key = jax.random.fold_in(key, 5)
    return 0.5 * jnp.clip(jax.random.normal(key, (M,), jnp.float32), -6.0, 6.0)


def steps_of(stream_key, shape, pieces, smallest, largest):
    loudness = 1.0
    for position, blocks in pieces:
        heights = jax.random.uniform(jax.random.fold_in(jax.random.fold_in(stream_key, 6), position), (blocks,), jnp.float32, smallest / len(pieces), largest / len(pieces))
        loudness = loudness * jnp.repeat(jnp.exp(heights), shape[position] // blocks).reshape((-1,) + (1,) * (len(shape) - 1 - position))
    return loudness


def setup_inputs(seed: int = 0) -> dict:
    splits = jax.random.split(jax.random.key(seed), 6)
    row_points = draw_row_points(jax.random.fold_in(splits[5], 71), 0)
    col_points = draw_col_points(jax.random.fold_in(splits[5], 71), 0)
    row_logmass = jnp.clip(jax.random.uniform(splits[2], (N,), jnp.float32, -4.0, 4.0) * steps_of(splits[2], (N,), ((0, 128),), -0.4, 0.0), -4.0, 4.0).astype(jnp.bfloat16)
    col_logmass = jnp.clip(jax.random.uniform(splits[3], (M,), jnp.float32, -4.0, 4.0) * steps_of(splits[3], (M,), ((0, 32),), -0.4, 0.0), -4.0, 4.0)
    col_potential = draw_col_potential(jax.random.fold_in(splits[5], 71), 0)
    return {"row_points": row_points, "col_points": col_points, "row_logmass": row_logmass, "col_logmass": col_logmass, "col_potential": col_potential}


epsilon = 0.05


def reference(row_points, col_points, row_logmass, col_logmass, col_potential):
    col_wide = col_points.astype(jnp.float32)
    col_norm = jnp.sum(col_wide * col_wide, axis=1)
    row_wide = row_points.astype(jnp.float32)
    row_norm = jnp.sum(row_wide * row_wide, axis=1)
    span = 1024 if N % 1024 == 0 else N
    blocks = N // span

    def block_cost(points_in, norms_in):
        cross = jnp.dot(points_in, col_points.T, preferred_element_type=jnp.float32)
        return norms_in[:, None] + col_norm[None, :] - 2.0 * cross

    def forward_block(pair):
        sq_cost = block_cost(pair[0], pair[1])
        scores = (col_potential[None, :] - sq_cost) / epsilon + col_logmass[None, :]
        highest = jnp.max(scores, axis=1)
        totals = jnp.sum(jnp.exp(scores - highest[:, None]), axis=1)
        return -epsilon * (highest + jnp.log(totals))

    row_potential = lax.map(forward_block, (row_points.reshape(blocks, span, DIM), row_norm.reshape(blocks, span))).reshape(N)

    def backward_block(running, quad):
        sq_cost = block_cost(quad[0], quad[1])
        scores = (quad[2][:, None] - sq_cost) / epsilon + quad[3].astype(jnp.float32)[:, None]
        new_peak = jnp.maximum(running[0], jnp.max(scores, axis=0))
        new_total = running[1] * jnp.exp(running[0] - new_peak) + jnp.sum(jnp.exp(scores - new_peak[None, :]), axis=0)
        return (new_peak, new_total), None

    start_state = (jnp.full((M,), -jnp.inf, jnp.float32), jnp.zeros((M,), jnp.float32))
    final_state, unused = lax.scan(backward_block, start_state, (row_points.reshape(blocks, span, DIM), row_norm.reshape(blocks, span), row_potential.reshape(blocks, span), row_logmass.reshape(blocks, span)))
    new_col_potential = -epsilon * (final_state[0] + jnp.log(final_state[1]))
    return row_potential, new_col_potential
```

```python
import jax
import jax.numpy as jnp
from jax import lax
from jax.experimental import pallas as pl
from jax.experimental.pallas import tpu as pltpu
from jax.sharding import Mesh
from jax.sharding import PartitionSpec as P

epsilon = 0.05
dim = 64
rows_own = 768
cols_own = 1024
peers = 8
zs = 4
depth = 80
ln2 = 0.6931471805599453
kappa = 40.0 / ln2
margin = 80.0
chunk = 256
finite_max = 3.0e38


def split3(v):
    first = v.astype(jnp.bfloat16)
    rest = v - first.astype(jnp.float32)
    second = rest.astype(jnp.bfloat16)
    third = (rest - second.astype(jnp.float32)).astype(jnp.bfloat16)
    return first, second, third


def place(rows, width):
    index = lax.broadcasted_iota(jnp.int32, (16, width), 0)
    block = jnp.zeros((16, width), jnp.float32)
    for at, row in rows:
        block = jnp.where(index == at, jnp.broadcast_to(row, (16, width)), block)
    return block.astype(jnp.bfloat16)


def prepare_kernel(x, mass, y, pot, logmass, rows_out, cols_out):
    one_r = jnp.ones((1, rows_own), jnp.float32)
    one_c = jnp.ones((1, cols_own), jnp.float32)
    rows_out[0:dim, :] = x[...]
    rows_out[dim:depth, :] = place(
        [(0, one_r), (1, one_r), (2, one_r), (6, mass[...].astype(jnp.float32))], rows_own
    )
    yw = y[...].astype(jnp.float32)
    norm = jnp.sum(yw * yw, axis=0, keepdims=True)
    c = 0.5 * (pot[...] - norm) + (0.5 * epsilon) * logmass[...]
    c1, c2, c3 = split3(c)
    cols_out[0:dim, :] = y[...]
    cols_out[dim:depth, :] = place(
        [(0, c1.astype(jnp.float32)), (1, c2.astype(jnp.float32)), (2, c3.astype(jnp.float32)),
         (3, one_c), (4, one_c), (5, one_c)], cols_own
    )


def score(left, right):
    return lax.dot_general(
        left, right, (((1,), (0,)), ((), ())), preferred_element_type=jnp.float32
    )


def forward_kernel(rows, cols, out, ys):
    width = rows_own
    total_cols = zs * cols_own
    for q in range(zs):
        for t in range(cols_own // 128):
            tile = cols[q, :, t * 128:(t + 1) * 128]
            tile = jnp.concatenate([tile, jnp.zeros((128 - depth, 128), jnp.bfloat16)], axis=0)
            ys[pl.ds(q * cols_own + t * 128, 128), :] = tile.T

    def block(b, carry):
        right = rows[b]
        sample = score(ys[0:128, 0:depth], right)
        shift = kappa * jnp.max(sample, axis=0, keepdims=True) + margin
        acc = jnp.zeros((8, width), jnp.float32)
        for u in range(total_cols // chunk):
            s = score(ys[u * chunk:(u + 1) * chunk, 0:depth], right)
            p = jnp.exp2(s * kappa - shift)
            acc = acc + jnp.sum(p.reshape(chunk // 8, 8, width), axis=0)
        out[pl.ds(b, 1), :] = shift + jnp.log2(jnp.sum(acc, axis=0, keepdims=True))
        return carry

    lax.fori_loop(0, peers, block, 0)

    @pl.when(jnp.logical_not(jnp.max(out[...]) < finite_max))
    def _():
        def exact(b, carry):
            right = rows[b]

            def peak_step(u, peak):
                s = score(ys[pl.ds(pl.multiple_of(u * chunk, chunk), chunk), 0:depth], right)
                return jnp.maximum(peak, jnp.max(s, axis=0, keepdims=True))

            peak = lax.fori_loop(
                0, total_cols // chunk, peak_step, jnp.full((1, width), -finite_max, jnp.float32)
            )

            def sum_step(u, acc):
                s = score(ys[pl.ds(pl.multiple_of(u * chunk, chunk), chunk), 0:depth], right)
                return acc + jnp.sum(jnp.exp2((s - peak) * kappa), axis=0, keepdims=True)

            total = lax.fori_loop(
                0, total_cols // chunk, sum_step, jnp.zeros((1, width), jnp.float32)
            )
            out[pl.ds(b, 1), :] = kappa * peak + jnp.log2(total)
            return carry

        lax.fori_loop(0, peers, exact, 0)


def merge_kernel(parts, rows, potential, ready):
    peak = parts[0]
    for i in range(1, peers):
        peak = jnp.maximum(peak, parts[i])
    total = jnp.exp2(parts[0] - peak)
    for i in range(1, peers):
        total = total + jnp.exp2(parts[i] - peak)
    merged = peak + jnp.log2(total)
    for b in range(peers):
        xw = rows[b, 0:dim, :].astype(jnp.float32)
        norm = jnp.sum(xw * xw, axis=0, keepdims=True)
        mine = merged[b:b + 1, :]
        potential[b:b + 1, :] = norm - (epsilon * ln2) * mine
        extras = rows[b, dim:depth, :]
        mass = extras.astype(jnp.float32)[6:7, :]
        r1, r2, r3 = split3(mass * (0.5 * epsilon) - mine * (1.0 / kappa))
        one = jnp.ones((1, rows_own), jnp.float32)
        ready[b, 0:dim, :] = rows[b, 0:dim, :]
        ready[b, dim:depth, :] = place(
            [(0, one), (1, one), (2, one), (3, r1.astype(jnp.float32)),
             (4, r2.astype(jnp.float32)), (5, r3.astype(jnp.float32))], rows_own
        )


def backward_kernel(rows, ys, out, acc, shift):
    total_cols = zs * cols_own
    steps = total_cols // chunk
    for u in range(steps):
        at = slice(u * chunk, (u + 1) * chunk)
        s = score(ys[at, 0:depth], rows[0, :, 0:256])
        top = jnp.max(jnp.maximum(s[:, 0:128], s[:, 128:256]), axis=1, keepdims=True)
        shift[at, :] = jnp.broadcast_to(top * kappa + margin, (chunk, 128))
        acc[at, :] = jnp.zeros((chunk, 128), jnp.float32)

    def block(b, carry):
        right = rows[b]
        for u in range(steps):
            at = slice(u * chunk, (u + 1) * chunk)
            s = score(ys[at, 0:depth], right)
            base = shift[at, :]
            run = acc[at, :]
            for t in range(rows_own // 128):
                run = run + jnp.exp2(s[:, t * 128:(t + 1) * 128] * kappa - base)
            acc[at, :] = run
        return carry

    lax.fori_loop(0, peers, block, 0)

    def finish(u, worst):
        at = pl.ds(pl.multiple_of(u * 128, 128), 128)
        total = jnp.sum(acc[at, :], axis=1, keepdims=True)
        logs = shift[at, :] + jnp.log2(jnp.broadcast_to(total, (128, 128)))
        line = logs.T[0:1, :]
        out[pl.ds(u, 1), :] = line
        return jnp.maximum(worst, line)

    worst = lax.fori_loop(
        0, total_cols // 128, finish, jnp.full((1, 128), -finite_max, jnp.float32)
    )

    @pl.when(jnp.logical_not(jnp.max(worst) < finite_max))
    def _():
        def exact(u, carry):
            left = ys[pl.ds(pl.multiple_of(u * 128, 128), 128), 0:depth]

            def peak_step(b, peak):
                s = score(left, rows[b])
                return jnp.maximum(peak, jnp.max(s, axis=1, keepdims=True))

            peak = lax.fori_loop(
                0, peers, peak_step, jnp.full((128, 1), -finite_max, jnp.float32)
            )

            def sum_step(b, total):
                s = score(left, rows[b])
                return total + jnp.sum(jnp.exp2((s - peak) * kappa), axis=1, keepdims=True)

            total = lax.fori_loop(0, peers, sum_step, jnp.zeros((128, 1), jnp.float32))
            logs = jnp.broadcast_to(peak * kappa + jnp.log2(total), (128, 128))
            out[pl.ds(u, 1), :] = logs.T[0:1, :]
            return carry

        lax.fori_loop(0, total_cols // 128, exact, 0)


def final_kernel(parts, pot, logmass, out):
    values = parts[...]
    peak = jnp.max(values, axis=0, keepdims=True)
    total = jnp.sum(jnp.exp2(values - peak), axis=0, keepdims=True)
    merged = peak + jnp.log2(total)
    out[...] = pot[...] + epsilon * logmass[...] - (epsilon * ln2) * merged


def params(mib):
    return pltpu.CompilerParams(vmem_limit_bytes=mib << 20)


def to_all(value, axes, count):
    return lax.all_to_all(jnp.broadcast_to(value[None], (count,) + value.shape), axes, 0, 0)


def body(row_points, col_points, row_logmass, col_logmass, col_potential):
    total_cols = zs * cols_own
    pot = col_potential.reshape(1, cols_own)
    mass_c = col_logmass.reshape(1, cols_own)
    rows_msg, cols_msg = pl.pallas_call(
        prepare_kernel,
        out_shape=(
            jax.ShapeDtypeStruct((depth, rows_own), jnp.bfloat16),
            jax.ShapeDtypeStruct((depth, cols_own), jnp.bfloat16),
        ),
        compiler_params=params(16),
        name="prepare",
    )(row_points.T, row_logmass.reshape(1, rows_own), col_points.T, pot, mass_c)
    rows = to_all(rows_msg, ("x", "k"), peers)
    cols = to_all(cols_msg, "z", zs)
    partial_rows, ys = pl.pallas_call(
        forward_kernel,
        out_shape=(
            jax.ShapeDtypeStruct((peers, rows_own), jnp.float32),
            jax.ShapeDtypeStruct((total_cols, 128), jnp.bfloat16),
        ),
        compiler_params=params(40),
        name="forward",
    )(rows, cols)
    parts = to_all(partial_rows, ("x", "k"), peers)
    potential, ready = pl.pallas_call(
        merge_kernel,
        out_shape=(
            jax.ShapeDtypeStruct((peers, rows_own), jnp.float32),
            jax.ShapeDtypeStruct((peers, depth, rows_own), jnp.bfloat16),
        ),
        compiler_params=params(16),
        name="merge_rows",
    )(parts, rows)
    row_potential = to_all(potential, "z", zs).reshape(-1)
    partial_cols = pl.pallas_call(
        backward_kernel,
        out_shape=jax.ShapeDtypeStruct((total_cols // 128, 128), jnp.float32),
        scratch_shapes=[
            pltpu.VMEM((total_cols, 128), jnp.float32),
            pltpu.VMEM((total_cols, 128), jnp.float32),
        ],
        compiler_params=params(40),
        name="backward",
    )(ready, ys)
    spread = jnp.tile(partial_cols.reshape(zs, cols_own), (4, 1))
    col_parts = lax.all_to_all(spread, ("y", "z"), 0, 0)
    new_col = pl.pallas_call(
        final_kernel,
        out_shape=jax.ShapeDtypeStruct((1, cols_own), jnp.float32),
        compiler_params=params(16),
        name="merge_cols",
    )(col_parts, pot, mass_c)
    return row_potential, new_col.reshape(cols_own)


def solution(mesh):
    fine = Mesh(mesh.devices.reshape(4, 4, 4, 2), ("y", "z", "x", "k"))
    cols = ("z", "x", "k")
    every = ("y",) + cols
    return jax.shard_map(
        body,
        mesh=fine,
        in_specs=(P(every, None), P(cols, None), P(every), P(cols), P(cols)),
        out_specs=(P("y"), P(cols)),
        check_vma=False,
    )
```

```python
import functools

import jax
import jax.numpy as jnp
from jax import lax
from jax.experimental import pallas as pl
from jax.experimental.pallas import tpu as pltpu
from jax.sharding import Mesh
from jax.sharding import PartitionSpec as P

epsilon = 0.05
dim = 64
rows_own = 768
cols_own = 1024
ring = 4
depth = 80
ln2 = 0.6931471805599453
kappa = 40.0 / ln2
margin = 80.0
chunk = 256
finite_max = 3.0e38
sampled = 64
row_lines = rows_own // 128
row_message = 32
offsets = (0, 1, 3, 2)


def split3(v):
    first = v.astype(jnp.bfloat16)
    rest = v - first.astype(jnp.float32)
    second = rest.astype(jnp.bfloat16)
    third = (rest - second.astype(jnp.float32)).astype(jnp.bfloat16)
    return [p.astype(jnp.float32) for p in (first, second, third)]


def place(rows, width):
    index = lax.broadcasted_iota(jnp.int32, (16, width), 0)
    block = jnp.zeros((16, width), jnp.float32)
    for at, row in enumerate(rows):
        block = jnp.where(index == at, jnp.broadcast_to(row, (16, width)), block)
    return block.astype(jnp.bfloat16)


def turned(tile):
    pad = jnp.zeros((128 - depth, 128), jnp.bfloat16)
    return jnp.concatenate([tile, pad], axis=0).T


def score(left, right):
    return lax.dot_general(
        left, right, (((1,), (0,)), ((), ())), preferred_element_type=jnp.float32
    )


def sampled_shift(left, right):
    sample = score(left[0:sampled, 0:depth], right)
    return kappa * jnp.max(sample, axis=0, keepdims=True) + margin


def shifted_sum(left, right, shift, count):
    width = right.shape[1]
    acc = jnp.zeros((8, width), jnp.float32)
    for u in range(count // chunk):
        s = score(left[u * chunk:(u + 1) * chunk, 0:depth], right)
        p = jnp.exp2(s * kappa - shift)
        acc = acc + jnp.sum(p.reshape(chunk // 8, 8, width), axis=0)
    return jnp.sum(acc, axis=0, keepdims=True)


def exact_log(lefts, right):
    width = right.shape[1]
    peak = jnp.full((1, width), -finite_max, jnp.float32)
    total = jnp.zeros((1, width), jnp.float32)

    def rows_at(left, u):
        return left[pl.ds(pl.multiple_of(u * chunk, chunk), chunk), 0:depth]

    for left in lefts:
        def peak_step(u, peak, left=left):
            return jnp.maximum(peak, jnp.max(score(rows_at(left, u), right), axis=0, keepdims=True))

        peak = lax.fori_loop(0, left.shape[0] // chunk, peak_step, peak)
    for left in lefts:
        def sum_step(u, total, left=left):
            s = score(rows_at(left, u), right)
            return total + jnp.sum(jnp.exp2((s - peak) * kappa), axis=0, keepdims=True)

        total = lax.fori_loop(0, left.shape[0] // chunk, sum_step, total)
    return kappa * peak + jnp.log2(total)


def prepare_kernel(y, pot, logmass, cols_out):
    one = jnp.ones((1, cols_own), jnp.float32)
    yw = y[...].astype(jnp.float32)
    norm = jnp.sum(yw * yw, axis=0, keepdims=True)
    c = 0.5 * (pot[...] - norm) + (0.5 * epsilon) * logmass[...]
    cols_out[0:dim, :] = y[...]
    cols_out[dim:depth, :] = place(split3(c) + [one, one, one], cols_own)


def put(out, at, line):
    for t in range(line.shape[1] // 128):
        out[at + t:at + t + 1, :] = line[:, t * 128:(t + 1) * 128]


def log_add(*terms):
    peak = terms[0]
    for t in terms[1:]:
        peak = jnp.maximum(peak, t)
    total = jnp.exp2(terms[0] - peak)
    for t in terms[1:]:
        total = total + jnp.exp2(t - peak)
    return peak + jnp.log2(total)


def line_of(ref, at, count):
    return jnp.concatenate([ref[at + t:at + t + 1, :] for t in range(count)], axis=1)


def forward_kernel(n_rows, n_cols, n_turned, n_old, n_mass, *refs):
    refs = list(refs)
    take = lambda n: [refs.pop(0) for _ in range(n)]
    rows, cols, lefts, olds, mass = take(n_rows), take(n_cols), take(n_turned), take(n_old), take(n_mass)
    out = refs.pop(0)
    if cols:
        ys = refs.pop(0)
        for q, col in enumerate(cols):
            for t in range(cols_own // 128):
                ys[q * cols_own + t * 128:q * cols_own + (t + 1) * 128, :] = turned(
                    col[:, t * 128:(t + 1) * 128]
                )
        lefts = lefts + [ys]
    one = jnp.ones((1, rows_own), jnp.float32)
    extras = place([one, one, one], rows_own)
    earlier = [(old, at) for old in olds for at in range(0, old.shape[0], row_lines)]
    for b, row in enumerate(rows):
        right = jnp.concatenate([row[...], extras], axis=0)
        if olds:
            shift = line_of(*earlier[b], row_lines) + margin
            total = 2.0 ** -margin
        else:
            shift = sampled_shift(lefts[0], right)
            total = 0.0
        for left in lefts:
            total = total + shifted_sum(left, right, shift, left.shape[0])
        put(out, b * row_lines, shift + jnp.log2(total))

    logs = slice(0, n_rows * row_lines)

    @pl.when(jnp.logical_not(jnp.max(out[logs, :]) < finite_max))
    def _():
        for b, row in enumerate(rows):
            right = jnp.concatenate([row[...], extras], axis=0)
            put(out, b * row_lines, exact_log(lefts, right))
            if olds:
                old, at = earlier[b]
                here = slice(b * row_lines, (b + 1) * row_lines)
                out[here, :] = log_add(old[at:at + row_lines, :], out[here, :])

    if mass:
        put(out, ring * row_lines, mass[0][...].astype(jnp.float32))
        out[(ring + 1) * row_lines:, :] = jnp.zeros((row_message - (ring + 1) * row_lines, 128), jnp.float32)


def merge_rows_kernel(place_x, own, far1, far3, far2, x0, x1, x3, x2, potential, ready):
    fars, points = (own, far1, far3, far2), (x0, x1, x3, x2)
    one = jnp.ones((1, rows_own), jnp.float32)
    found = []
    for b in range(ring):
        lines = [(b ^ d) * row_lines for d in range(ring)]
        merged = log_add(*[far[n:n + row_lines, :] for n, far in zip(lines, fars)])
        at = ring * row_lines
        mass = fars[b][at:at + row_lines, :]
        xw = points[b][...].astype(jnp.float32)
        norm = jnp.sum(xw * xw, axis=0, keepdims=True)
        norm = jnp.concatenate([norm[:, t * 128:(t + 1) * 128] for t in range(row_lines)], axis=0)
        found.append(norm - (epsilon * ln2) * merged)
        r = mass * (0.5 * epsilon) - merged * (1.0 / kappa)
        tall = jnp.concatenate(
            [points[b][...], place([one, one, one] + split3(line_of(r, 0, row_lines)), rows_own)], axis=0
        )
        for t in range(row_lines):
            at = b * rows_own + t * 128
            ready[at:at + 128, :] = turned(tall[:, t * 128:(t + 1) * 128])
    x = place_x[0]
    for index in range(ring):
        value = found[offsets.index(index)]
        for other in range(1, ring):
            value = jnp.where(x == other, found[offsets.index(index ^ other)], value)
        potential[index * row_lines:(index + 1) * row_lines, :] = value


def column_logs(xs, cols, logs):
    for q, col in enumerate(cols):
        right = col[...]
        shift = sampled_shift(xs, right)
        put(logs, q * 8, shift + jnp.log2(shifted_sum(xs, right, shift, ring * rows_own)))

    @pl.when(jnp.logical_not(jnp.max(logs[0:len(cols) * 8, :]) < finite_max))
    def _():
        for q, col in enumerate(cols):
            put(logs, q * 8, exact_log([xs], col[...]))


def backward_kernel(xs, *refs):
    column_logs(xs, refs[:-1], refs[-1])


def to_core_kernel(logs, potential, out):
    out[0:32, :] = logs[...]
    out[32:56, :] = potential[...]


def backward_last_kernel(place_z, xs, c3, c2, early, swapped, out, logs):
    column_logs(xs, (c3, c2), logs)
    for p, d in enumerate(offsets):
        mine = (early if p < 2 else logs)[p % 2 * 8:(p % 2 + 1) * 8, :]
        value = log_add(mine, swapped[p * 8:(p + 1) * 8, :])
        for y in range(ring):
            out[y * ring + (place_z[0] ^ d)] = value


def pack_kernel(core, mine, theirs, out):
    first = core[0] == 0
    for x in range(ring):
        a = mine[32 + x * row_lines:32 + (x + 1) * row_lines, :]
        b = theirs[32 + x * row_lines:32 + (x + 1) * row_lines, :]
        at = 2 * x * row_lines
        out[at:at + row_lines, :] = jnp.where(first, a, b)
        out[at + row_lines:at + 2 * row_lines, :] = jnp.where(first, b, a)


def pack_two_kernel(mine, far, out):
    out[0:48, :] = mine[...]
    out[48:96, :] = far[...]


def order_kernel(place_z, mine, near, out):
    z = place_z[0]
    for other, ref, at in ((0, mine, 0), (3, mine, 48), (1, near, 0), (2, near, 48)):
        out[pl.ds(pl.multiple_of((z ^ other) * 48, 8), 48), :] = ref[at:at + 48, :]


def final_kernel(parts, pot, logmass, out):
    merged = log_add(*[parts[i] for i in range(ring * ring)])
    out[...] = pot[...] + epsilon * logmass[...] - (epsilon * ln2) * merged


def call(kernel, name, out, args, mib=24, pairs=0, scratch=(), scalars=0, last=False):
    within = {} if last else {"out_specs": jax.tree.map(lambda _: pl.BlockSpec(memory_space=pltpu.VMEM), out)}
    specs = [pl.BlockSpec(memory_space=pltpu.SMEM)] * scalars
    specs += [pl.BlockSpec(memory_space=pltpu.VMEM)] * (len(args) - scalars)
    return pl.pallas_call(
        kernel,
        out_shape=out,
        in_specs=specs,
        **within,
        scratch_shapes=list(scratch),
        compiler_params=pltpu.CompilerParams(vmem_limit_bytes=mib << 20),
        cost_estimate=pl.CostEstimate(flops=pairs * 512, bytes_accessed=1 << 20, transcendentals=pairs),
        name=name,
    )(*args)


def across(value, axis, bits):
    return lax.ppermute(value, axis, [(i, i ^ bits) for i in range(ring)])


def swap(value):
    return lax.ppermute(value, "k", [(0, 1), (1, 0)])


def after(value, *earlier):
    return lax.optimization_barrier((value, *earlier))[0]


def shape(*dims, dtype=jnp.float32):
    return jax.ShapeDtypeStruct(dims, dtype)


def index_of(axis):
    return lax.axis_index(axis).astype(jnp.int32).reshape(1)


def forward(rows, cols=(), lefts=(), olds=(), mass=()):
    outs = [shape(row_message if mass else len(rows) * row_lines, 128)]
    turned_cols = (len(cols) * cols_own, 128)
    scratch = [pltpu.VMEM(turned_cols, jnp.bfloat16)] if mass else []
    if cols and not mass:
        outs.append(shape(*turned_cols, dtype=jnp.bfloat16))
    kernel = functools.partial(forward_kernel, len(rows), len(cols), len(lefts), len(olds), len(mass))
    pairs = len(rows) * rows_own * (len(cols) + 2 * len(lefts)) * cols_own
    return call(kernel, "forward", tuple(outs), (*rows, *cols, *lefts, *olds, *mass), pairs=pairs, scratch=scratch)


def body(row_points, col_points, row_logmass, col_logmass, col_potential):
    mass_r = row_logmass.reshape(1, rows_own)
    mine = row_points.T
    x1, x3 = (across(mine, "x", d) for d in (1, 3))
    own = call(
        prepare_kernel, "prepare", shape(depth, cols_own, dtype=jnp.bfloat16),
        (col_points.T, col_potential.reshape(1, cols_own), col_logmass.reshape(1, cols_own)),
    )
    z1, z3 = (across(own, "z", d) for d in (1, 3))
    over0 = swap(own)
    some = (mine, x1, x3)
    logs, ys0 = forward(some, (own, over0))
    x2 = across(after(x1, logs), "x", 3)
    z2 = across(after(z1, logs), "z", 3)
    over1, over3 = swap(after(z1, logs)), swap(after(z3, logs))
    logs, ys1 = forward(some, (z1, z3), olds=(logs,))
    over1, over3, _ = lax.optimization_barrier((over1, over3, logs))
    logs, ys2 = forward(some, (over1, over3), olds=(logs,))
    x2 = after(x2, logs)
    logs2 = forward((x2,), lefts=(ys0, ys1, ys2))[0]
    over2 = swap(after(z2, logs))
    over2 = after(over2, logs2)
    logs = forward((*some, x2), (z2, over2), olds=(logs, logs2), mass=(mass_r,))[0]

    fars = [across(logs, "x", d) for d in (1, 3, 2)]
    potential, ready = call(
        merge_rows_kernel, "merge_rows",
        (shape(ring * row_lines, 128), shape(ring * rows_own, 128, dtype=jnp.bfloat16)),
        (index_of("x"), logs, *fars, *some, x2), scalars=1,
    )

    block = ring * rows_own * cols_own
    other = call(
        backward_kernel, "backward", shape(32, 128), (ready, over0, over1, over3, over2), pairs=4 * block
    )
    to_core = call(to_core_kernel, "to_core", shape(56, 128), (other, potential))
    swapped = swap(to_core)
    early = call(backward_kernel, "backward", shape(16, 128), (after(ready, to_core), own, z1), pairs=2 * block)
    swapped = after(swapped, early)
    chip = call(pack_kernel, "pack", shape(48, 128), (index_of("k"), to_core, swapped), scalars=1)
    far = across(chip, "z", 3)
    sums = call(
        backward_last_kernel, "backward_last", shape(ring * ring, 8, 128),
        (index_of("z"), ready, z3, z2, early, swapped),
        pairs=2 * block, scratch=[pltpu.VMEM((16, 128), jnp.float32)], scalars=1,
    )
    parts = lax.all_to_all(sums, ("y", "z"), 0, 0)
    chips = call(pack_two_kernel, "pack_two", shape(96, 128), (chip, after(far, sums)))
    row_potential = call(
        order_kernel, "order", shape(ring * 48, 128), (index_of("z"), chips, across(chips, "z", 1)), scalars=1, last=True,
    )
    new_col = call(
        final_kernel, "merge_cols", shape(8, 128),
        (parts, col_potential.reshape(8, 128), col_logmass.reshape(8, 128)), last=True,
    )
    return row_potential.reshape(-1), new_col.reshape(cols_own)


def solution(mesh):
    fine = Mesh(mesh.devices.reshape(ring, ring, ring, 2), ("y", "z", "x", "k"))
    cols = ("z", "x", "k")
    every = ("y",) + cols
    return jax.shard_map(
        body,
        mesh=fine,
        in_specs=(P(every, None), P(cols, None), P(every), P(cols), P(cols)),
        out_specs=(P("y"), P(cols)),
        check_vma=False,
    )
```

```python
import functools

import jax
import jax.numpy as jnp
from jax import lax
from jax.experimental import pallas as pl
from jax.experimental.pallas import tpu as pltpu
from jax.sharding import Mesh
from jax.sharding import PartitionSpec as P

epsilon = 0.05
dim = 64
rows_own = 768
cols_own = 1024
ring = 4
depth = 80
ln2 = 0.6931471805599453
kappa = 40.0 / ln2
margin = 80.0
chunk = 256
careful = 64
finite_max = 3.0e38
sampled = 64
row_lines = rows_own // 128
offsets = (0, 1, 3, 2)


def split3(v):
    first = v.astype(jnp.bfloat16)
    rest = v - first.astype(jnp.float32)
    second = rest.astype(jnp.bfloat16)
    third = (rest - second.astype(jnp.float32)).astype(jnp.bfloat16)
    return [p.astype(jnp.float32) for p in (first, second, third)]


def place(rows, width):
    index = lax.broadcasted_iota(jnp.int32, (16, width), 0)
    block = jnp.zeros((16, width), jnp.float32)
    for at, row in enumerate(rows):
        block = jnp.where(index == at, jnp.broadcast_to(row, (16, width)), block)
    return block.astype(jnp.bfloat16)


def turned(tile):
    pad = jnp.zeros((128 - depth, 128), jnp.bfloat16)
    return jnp.concatenate([tile, pad], axis=0).T


def score(left, right):
    return lax.dot_general(
        left, right, (((1,), (0,)), ((), ())), preferred_element_type=jnp.float32
    )


def sampled_shift(left, right):
    sample = score(left[0:sampled, 0:depth], right)
    return kappa * jnp.max(sample, axis=0, keepdims=True) + margin


def shifted_sum(left, right, shift, count):
    width = right.shape[1]
    acc = jnp.zeros((8, width), jnp.float32)
    for u in range(count // chunk):
        s = score(left[u * chunk:(u + 1) * chunk, 0:depth], right)
        p = jnp.exp2(s * kappa - shift)
        acc = acc + jnp.sum(p.reshape(chunk // 8, 8, width), axis=0)
    return jnp.sum(acc, axis=0, keepdims=True)


def exact_log(lefts, right):
    width = right.shape[1]
    peak = jnp.full((1, width), -finite_max, jnp.float32)
    total = jnp.zeros((1, width), jnp.float32)

    def rows_at(left, u):
        return left[pl.ds(pl.multiple_of(u * careful, careful), careful), 0:depth]

    for left in lefts:
        def peak_step(u, peak, left=left):
            return jnp.maximum(peak, jnp.max(score(rows_at(left, u), right), axis=0, keepdims=True))

        peak = lax.fori_loop(0, left.shape[0] // careful, peak_step, peak)
    for left in lefts:
        def sum_step(u, total, left=left):
            s = score(rows_at(left, u), right)
            return total + jnp.sum(jnp.exp2((s - peak) * kappa), axis=0, keepdims=True)

        total = lax.fori_loop(0, left.shape[0] // careful, sum_step, total)
    return kappa * peak + jnp.log2(total)


def prepare_kernel(y, pot, logmass, cols_out):
    one = jnp.ones((1, cols_own), jnp.float32)
    yw = y[...].astype(jnp.float32)
    norm = jnp.sum(yw * yw, axis=0, keepdims=True)
    c = 0.5 * (pot[...] - norm) + (0.5 * epsilon) * logmass[...]
    cols_out[0:dim, :] = y[...]
    cols_out[dim:depth, :] = place(split3(c) + [one, one, one], cols_own)


def to_lines(line):
    count = line.shape[1] // 128
    parts = [line[:, t * 128:(t + 1) * 128] for t in range(count)]
    if count < 8:
        parts.append(jnp.zeros((8 - count, 128), jnp.float32))
    return jnp.concatenate(parts, axis=0)


def eight(at):
    return pl.ds(pl.multiple_of(at * 8, 8), 8)


def log_add(*terms):
    peak = terms[0]
    for t in terms[1:]:
        peak = jnp.maximum(peak, t)
    total = jnp.exp2(terms[0] - peak)
    for t in terms[1:]:
        total = total + jnp.exp2(t - peak)
    return peak + jnp.log2(total)


def line_of(lines, count):
    return jnp.concatenate([lines[t:t + 1, :] for t in range(count)], axis=1)


def forward_kernel(n_rows, n_cols, n_turned, n_old, n_mass, *refs):
    refs = list(refs)
    take = lambda n: [refs.pop(0) for _ in range(n)]
    rows, cols, lefts, olds, mass = take(n_rows), take(n_cols), take(n_turned), take(n_old), take(n_mass)
    out = refs.pop(0)
    stack = refs.pop(-1)
    if cols:
        ys = refs.pop(0)
        for q, col in enumerate(cols):
            def turn(t, carry, q=q, col=col):
                at = pl.multiple_of(t * 128, 128)
                ys[pl.ds(pl.multiple_of(q * cols_own + at, 128), 128), :] = turned(col[:, pl.ds(at, 128)])
                return carry

            lax.fori_loop(0, cols_own // 128, turn, 0, unroll=4)
        lefts = lefts + [ys]
    one = jnp.ones((1, rows_own), jnp.float32)
    extras = place([one, one, one], rows_own)
    for b, row in enumerate(rows):
        stack[b, 0:dim, :] = row[...]
        stack[b, dim:depth, :] = extras
    at = 0
    for old in olds:
        out[at:at + old.shape[0], :] = old[...]
        at += old.shape[0]

    def block(b, worst):
        right = stack[b]
        if olds:
            shift = line_of(out[eight(b), :], row_lines) + margin
            total = 2.0 ** -margin
        else:
            shift = sampled_shift(lefts[0], right)
            total = 0.0
        for left in lefts:
            total = total + shifted_sum(left, right, shift, left.shape[0])
        logs = shift + jnp.log2(total)
        out[eight(b), :] = to_lines(logs)
        return jnp.maximum(worst, logs)

    worst = lax.fori_loop(0, n_rows, block, jnp.full((1, rows_own), -finite_max, jnp.float32))

    @pl.when(jnp.logical_not(jnp.max(worst) < finite_max))
    def _():
        at = 0
        for old in olds:
            out[at:at + old.shape[0], :] = old[...]
            at += old.shape[0]

        def exact(b, carry):
            logs = to_lines(exact_log(lefts, stack[b]))
            out[eight(b), :] = log_add(out[eight(b), :], logs) if olds else logs
            return carry

        lax.fori_loop(0, n_rows, exact, 0)

    if mass:
        out[ring * 8:(ring + 1) * 8, :] = to_lines(mass[0][...].astype(jnp.float32))


def merge_rows_kernel(place_x, own, far1, far3, far2, x0, x1, x3, x2, potential, ready):
    fars, points = (own, far1, far3, far2), (x0, x1, x3, x2)
    one = jnp.ones((1, rows_own), jnp.float32)
    found = []
    for b in range(ring):
        lines = [(b ^ d) * 8 for d in range(ring)]
        merged = log_add(*[far[n:n + row_lines, :] for n, far in zip(lines, fars)])
        mass = fars[b][ring * 8:ring * 8 + row_lines, :]
        xw = points[b][...].astype(jnp.float32)
        norm = jnp.sum(xw * xw, axis=0, keepdims=True)
        norm = jnp.concatenate([norm[:, t * 128:(t + 1) * 128] for t in range(row_lines)], axis=0)
        found.append(norm - (epsilon * ln2) * merged)
        r = mass * (0.5 * epsilon) - merged * (1.0 / kappa)
        tall = jnp.concatenate(
            [points[b][...], place([one, one, one] + split3(line_of(r, row_lines)), rows_own)], axis=0
        )
        for t in range(row_lines):
            at = b * rows_own + t * 128
            ready[at:at + 128, :] = turned(tall[:, t * 128:(t + 1) * 128])
    x = place_x[0]
    for index in range(ring):
        value = found[offsets.index(index)]
        for other in range(1, ring):
            value = jnp.where(x == other, found[offsets.index(index ^ other)], value)
        potential[index * row_lines:(index + 1) * row_lines, :] = value


def column_logs(xs, cols, logs, stack):
    for q, col in enumerate(cols):
        stack[q] = col[...]

    def block(q, worst):
        right = stack[q]
        shift = sampled_shift(xs, right)
        found = shift + jnp.log2(shifted_sum(xs, right, shift, ring * rows_own))
        logs[eight(q), :] = to_lines(found)
        return jnp.maximum(worst, found)

    worst = lax.fori_loop(0, len(cols), block, jnp.full((1, cols_own), -finite_max, jnp.float32))

    @pl.when(jnp.logical_not(jnp.max(worst) < finite_max))
    def _():
        def exact(q, carry):
            logs[eight(q), :] = to_lines(exact_log([xs], stack[q]))
            return carry

        lax.fori_loop(0, len(cols), exact, 0)


def backward_kernel(xs, *refs):
    column_logs(xs, refs[:-2], refs[-2], refs[-1])


def to_core_kernel(logs, potential, out):
    out[0:32, :] = logs[...]
    out[32:56, :] = potential[...]


def backward_last_kernel(place_z, xs, c3, c2, early, swapped, out, logs, stack):
    column_logs(xs, (c3, c2), logs, stack)
    for p, d in enumerate(offsets):
        mine = (early if p < 2 else logs)[p % 2 * 8:(p % 2 + 1) * 8, :]
        value = log_add(mine, swapped[p * 8:(p + 1) * 8, :])
        for y in range(ring):
            out[y * ring + (place_z[0] ^ d)] = value


def pack_kernel(core, mine, theirs, out):
    first = core[0] == 0
    for x in range(ring):
        a = mine[32 + x * row_lines:32 + (x + 1) * row_lines, :]
        b = theirs[32 + x * row_lines:32 + (x + 1) * row_lines, :]
        at = 2 * x * row_lines
        out[at:at + row_lines, :] = jnp.where(first, a, b)
        out[at + row_lines:at + 2 * row_lines, :] = jnp.where(first, b, a)


def pack_two_kernel(mine, far, out):
    out[0:48, :] = mine[...]
    out[48:96, :] = far[...]


def final_kernel(place_z, parts, pot, logmass, mine, near, out, potential):
    merged = log_add(*[parts[i] for i in range(ring * ring)])
    out[...] = pot[...] + epsilon * logmass[...] - (epsilon * ln2) * merged
    z = place_z[0]
    for other, ref, at in ((0, mine, 0), (3, mine, 48), (1, near, 0), (2, near, 48)):
        potential[pl.ds(pl.multiple_of((z ^ other) * 48, 8), 48), :] = ref[at:at + 48, :]


def call(kernel, name, out, args, mib=24, pairs=0, scratch=(), scalars=0, last=False):
    within = {} if last else {"out_specs": jax.tree.map(lambda _: pl.BlockSpec(memory_space=pltpu.VMEM), out)}
    specs = [pl.BlockSpec(memory_space=pltpu.SMEM)] * scalars
    specs += [pl.BlockSpec(memory_space=pltpu.VMEM)] * (len(args) - scalars)
    return pl.pallas_call(
        kernel,
        out_shape=out,
        in_specs=specs,
        **within,
        scratch_shapes=list(scratch),
        compiler_params=pltpu.CompilerParams(vmem_limit_bytes=mib << 20),
        cost_estimate=pl.CostEstimate(flops=pairs * 512, bytes_accessed=1 << 20, transcendentals=pairs),
        name=name,
    )(*args)


def across(value, axis, bits):
    return lax.ppermute(value, axis, [(i, i ^ bits) for i in range(ring)])


def swap(value):
    return lax.ppermute(value, "k", [(0, 1), (1, 0)])


def after(value, *earlier):
    return lax.optimization_barrier((value, *earlier))[0]


def shape(*dims, dtype=jnp.float32):
    return jax.ShapeDtypeStruct(dims, dtype)


def index_of(axis):
    return lax.axis_index(axis).astype(jnp.int32).reshape(1)


def stack_of(count, *dims):
    return pltpu.VMEM((count, depth, *dims), jnp.bfloat16)


def forward(rows, cols=(), lefts=(), olds=(), mass=()):
    outs = [shape(8 * len(rows) + (8 if mass else 0), 128)]
    turned_cols = (len(cols) * cols_own, 128)
    scratch = [pltpu.VMEM(turned_cols, jnp.bfloat16)] if mass else []
    if cols and not mass:
        outs.append(shape(*turned_cols, dtype=jnp.bfloat16))
    kernel = functools.partial(forward_kernel, len(rows), len(cols), len(lefts), len(olds), len(mass))
    pairs = len(rows) * rows_own * (len(cols) + 2 * len(lefts)) * cols_own
    return call(
        kernel, "forward", tuple(outs), (*rows, *cols, *lefts, *olds, *mass), pairs=pairs,
        scratch=scratch + [stack_of(len(rows), rows_own)],
    )


def body(row_points, col_points, row_logmass, col_logmass, col_potential):
    mass_r = row_logmass.reshape(1, rows_own)
    mine = row_points.T
    x1, x3 = (across(mine, "x", d) for d in (1, 3))
    own = call(
        prepare_kernel, "prepare", shape(depth, cols_own, dtype=jnp.bfloat16),
        (col_points.T, col_potential.reshape(1, cols_own), col_logmass.reshape(1, cols_own)),
    )
    z1, z3 = (across(own, "z", d) for d in (1, 3))
    over0 = swap(own)
    some = (mine, x1, x3)
    logs, ys0 = forward(some, (own, over0))
    x2 = across(after(x1, logs), "x", 3)
    z2 = across(after(z1, logs), "z", 3)
    over1, over3 = swap(after(z1, logs)), swap(after(z3, logs))
    logs, ys1 = forward(some, (z1, z3), olds=(logs,))
    over1, over3, _ = lax.optimization_barrier((over1, over3, logs))
    logs, ys2 = forward(some, (over1, over3), olds=(logs,))
    x2 = after(x2, logs)
    logs2 = forward((x2,), lefts=(ys0, ys1, ys2))[0]
    over2 = swap(after(z2, logs))
    over2 = after(over2, logs2)
    logs = forward((*some, x2), (z2, over2), olds=(logs, logs2), mass=(mass_r,))[0]

    fars = [across(logs, "x", d) for d in (1, 3, 2)]
    potential, ready = call(
        merge_rows_kernel, "merge_rows",
        (shape(ring * row_lines, 128), shape(ring * rows_own, 128, dtype=jnp.bfloat16)),
        (index_of("x"), logs, *fars, *some, x2), scalars=1,
    )

    block = ring * rows_own * cols_own
    other = call(
        backward_kernel, "backward", shape(32, 128), (ready, over0, over1, over3, over2), pairs=4 * block,
        scratch=[stack_of(4, cols_own)],
    )
    to_core = call(to_core_kernel, "to_core", shape(56, 128), (other, potential))
    swapped = swap(to_core)
    early = call(backward_kernel, "backward", shape(16, 128), (after(ready, to_core), own, z1), pairs=2 * block, scratch=[stack_of(2, cols_own)])
    swapped = after(swapped, early)
    chip = call(pack_kernel, "pack", shape(48, 128), (index_of("k"), to_core, swapped), scalars=1)
    far = across(chip, "z", 3)
    sums = call(
        backward_last_kernel, "backward_last", shape(ring * ring, 8, 128),
        (index_of("z"), ready, z3, z2, early, swapped),
        pairs=2 * block, scratch=[pltpu.VMEM((16, 128), jnp.float32), stack_of(2, cols_own)], scalars=1,
    )
    parts = lax.all_to_all(sums, ("y", "z"), 0, 0)
    chips = call(pack_two_kernel, "pack_two", shape(96, 128), (chip, after(far, sums)))
    new_col, row_potential = call(
        final_kernel, "finish", (shape(8, 128), shape(ring * 48, 128)),
        (index_of("z"), parts, col_potential.reshape(8, 128), col_logmass.reshape(8, 128),
         chips, across(chips, "z", 1)), scalars=1, last=True,
    )
    return row_potential.reshape(-1), new_col.reshape(cols_own)


def solution(mesh):
    fine = Mesh(mesh.devices.reshape(ring, ring, ring, 2), ("y", "z", "x", "k"))
    cols = ("z", "x", "k")
    every = ("y",) + cols
    return jax.shard_map(
        body,
        mesh=fine,
        in_specs=(P(every, None), P(cols, None), P(every), P(cols), P(cols)),
        out_specs=(P("y"), P(cols)),
        check_vma=False,
    )
```

```python
import functools

import jax
import jax.numpy as jnp
from jax import lax
from jax.experimental import pallas as pl
from jax.experimental.pallas import tpu as pltpu
from jax.sharding import Mesh
from jax.sharding import PartitionSpec as P

epsilon = 0.05
dim = 64
rows_own = 768
cols_own = 1024
ring = 4
depth = 80
ln2 = 0.6931471805599453
kappa = 40.0 / ln2
margin = 80.0
chunk = 256
careful = 64
finite_max = 3.0e38
sampled = 64
row_lines = rows_own // 128
offsets = (0, 1, 3, 2)


def split3(v):
    first = v.astype(jnp.bfloat16)
    rest = v - first.astype(jnp.float32)
    second = rest.astype(jnp.bfloat16)
    third = (rest - second.astype(jnp.float32)).astype(jnp.bfloat16)
    return [p.astype(jnp.float32) for p in (first, second, third)]


def place(rows, width):
    index = lax.broadcasted_iota(jnp.int32, (16, width), 0)
    block = jnp.zeros((16, width), jnp.float32)
    for at, row in enumerate(rows):
        block = jnp.where(index == at, jnp.broadcast_to(row, (16, width)), block)
    return block.astype(jnp.bfloat16)


def turned(tile):
    pad = jnp.zeros((128 - depth, 128), jnp.bfloat16)
    return jnp.concatenate([tile, pad], axis=0).T


def score(left, right):
    return lax.dot_general(
        left, right, (((1,), (0,)), ((), ())), preferred_element_type=jnp.float32
    )


def sampled_shift(left, right):
    sample = score(left[0:sampled, 0:depth], right)
    return kappa * jnp.max(sample, axis=0, keepdims=True) + margin


def shifted_sum(left, right, shift, count):
    width = right.shape[1]
    acc = jnp.zeros((8, width), jnp.float32)
    for u in range(count // chunk):
        s = score(left[u * chunk:(u + 1) * chunk, 0:depth], right)
        p = jnp.exp2(s * kappa - shift)
        acc = acc + jnp.sum(p.reshape(chunk // 8, 8, width), axis=0)
    return jnp.sum(acc, axis=0, keepdims=True)


def exact_log(lefts, right):
    width = right.shape[1]
    peak = jnp.full((1, width), -finite_max, jnp.float32)
    total = jnp.zeros((1, width), jnp.float32)

    def rows_at(left, u):
        return left[pl.ds(pl.multiple_of(u * careful, careful), careful), 0:depth]

    for left in lefts:
        def peak_step(u, peak, left=left):
            return jnp.maximum(peak, jnp.max(score(rows_at(left, u), right), axis=0, keepdims=True))

        peak = lax.fori_loop(0, left.shape[0] // careful, peak_step, peak)
    for left in lefts:
        def sum_step(u, total, left=left):
            s = score(rows_at(left, u), right)
            return total + jnp.sum(jnp.exp2((s - peak) * kappa), axis=0, keepdims=True)

        total = lax.fori_loop(0, left.shape[0] // careful, sum_step, total)
    return kappa * peak + jnp.log2(total)


def prepare_kernel(y_far, pot_far, logmass_far, cols_out, y, pot, logmass, done):
    copies = [
        pltpu.make_async_copy(source, target, done.at[i])
        for i, (source, target) in enumerate(((y_far, y), (pot_far, pot), (logmass_far, logmass)))
    ]
    for copy in copies:
        copy.start()
    for copy in copies:
        copy.wait()
    one = jnp.ones((1, cols_own), jnp.float32)
    yw = y[...].astype(jnp.float32)
    norm = jnp.sum(yw * yw, axis=0, keepdims=True)
    c = 0.5 * (pot[...] - norm) + (0.5 * epsilon) * logmass[...]
    cols_out[0:dim, :] = y[...]
    cols_out[dim:depth, :] = place(split3(c) + [one, one, one], cols_own)


def pair_kernel(core, mine, theirs, out):
    out[core[0]] = mine[...]
    out[1 - core[0]] = theirs[...]


def parcel_kernel(core, rows, cols, out):
    @pl.when(core[0] == 0)
    def _():
        out[...] = jnp.zeros(out.shape, jnp.bfloat16)
        out[:, 0:dim, 0:rows_own] = rows[...]

    @pl.when(core[0] == 1)
    def _():
        out[...] = cols[...]


def open_kernel(core, here, there, rows, cols):
    @pl.when(core[0] == 0)
    def _():
        rows[...] = here[0, 0:dim, 0:rows_own]
        cols[...] = there[...]

    @pl.when(core[0] == 1)
    def _():
        rows[...] = there[1, 0:dim, 0:rows_own]
        cols[...] = here[...]


def pick_kernel(core, pair, out):
    out[...] = pair[core[0]]


def to_lines(line):
    count = line.shape[1] // 128
    parts = [line[:, t * 128:(t + 1) * 128] for t in range(count)]
    if count < 8:
        parts.append(jnp.zeros((8 - count, 128), jnp.float32))
    return jnp.concatenate(parts, axis=0)


def eight(at):
    return pl.ds(pl.multiple_of(at * 8, 8), 8)


def log_add(*terms):
    peak = terms[0]
    for t in terms[1:]:
        peak = jnp.maximum(peak, t)
    total = jnp.exp2(terms[0] - peak)
    for t in terms[1:]:
        total = total + jnp.exp2(t - peak)
    return peak + jnp.log2(total)


def line_of(lines, count):
    return jnp.concatenate([lines[t:t + 1, :] for t in range(count)], axis=1)


def forward_kernel(n_rows, n_cols, n_turned, n_old, n_mass, *refs):
    refs = list(refs)
    take = lambda n: [refs.pop(0) for _ in range(n)]
    rows, cols, lefts, olds, mass = take(n_rows), take(n_cols), take(n_turned), take(n_old), take(n_mass)
    if n_cols == 1:
        cols = [cols[0].at[0], cols[0].at[1]]
    out = refs.pop(0)
    stack = refs.pop(-1)
    if cols:
        ys = refs.pop(0)
        for q, col in enumerate(cols):
            def turn(t, carry, q=q, col=col):
                at = pl.multiple_of(t * 128, 128)
                ys[pl.ds(pl.multiple_of(q * cols_own + at, 128), 128), :] = turned(col[:, pl.ds(at, 128)])
                return carry

            lax.fori_loop(0, cols_own // 128, turn, 0, unroll=4)
        lefts = lefts + [ys]
    one = jnp.ones((1, rows_own), jnp.float32)
    extras = place([one, one, one], rows_own)
    for b, row in enumerate(rows):
        stack[b, 0:dim, :] = row[...]
        stack[b, dim:depth, :] = extras
    at = 0
    for old in olds:
        out[at:at + old.shape[0], :] = old[...]
        at += old.shape[0]

    def block(b, worst):
        right = stack[b]
        if olds:
            shift = line_of(out[eight(b), :], row_lines) + margin
            total = 2.0 ** -margin
        else:
            shift = sampled_shift(lefts[0], right)
            total = 0.0
        for left in lefts:
            total = total + shifted_sum(left, right, shift, left.shape[0])
        logs = shift + jnp.log2(total)
        out[eight(b), :] = to_lines(logs)
        return jnp.maximum(worst, logs)

    worst = jnp.full((1, rows_own), -finite_max, jnp.float32)
    worst = lax.fori_loop(0, n_rows, block, worst, unroll=2 if n_rows == ring else 1)

    @pl.when(jnp.logical_not(jnp.max(worst) < finite_max))
    def _():
        at = 0
        for old in olds:
            out[at:at + old.shape[0], :] = old[...]
            at += old.shape[0]

        def exact(b, carry):
            logs = to_lines(exact_log(lefts, stack[b]))
            out[eight(b), :] = log_add(out[eight(b), :], logs) if olds else logs
            return carry

        lax.fori_loop(0, n_rows, exact, 0)

    if mass:
        out[ring * 8:(ring + 1) * 8, :] = to_lines(mass[0][...].astype(jnp.float32))


def merge_rows_kernel(place_x, core, own, far1, far3, far2, x0, x1, x3, x2, potential, ready):
    first = core[0] == 0
    near, far = far1[...], far3[...]
    fars = (own[...], jnp.where(first, near, far), jnp.where(first, far, near), far2[...])
    points = (x0, x1, x3, x2)
    one = jnp.ones((1, rows_own), jnp.float32)
    found = []
    for b in range(ring):
        lines = [(b ^ d) * 8 for d in range(ring)]
        merged = log_add(*[far[n:n + row_lines, :] for n, far in zip(lines, fars)])
        mass = fars[b][ring * 8:ring * 8 + row_lines, :]
        xw = points[b][...].astype(jnp.float32)
        norm = jnp.sum(xw * xw, axis=0, keepdims=True)
        norm = jnp.concatenate([norm[:, t * 128:(t + 1) * 128] for t in range(row_lines)], axis=0)
        found.append(norm - (epsilon * ln2) * merged)
        r = mass * (0.5 * epsilon) - merged * (1.0 / kappa)
        tall = jnp.concatenate(
            [points[b][...], place([one, one, one] + split3(line_of(r, row_lines)), rows_own)], axis=0
        )
        for t in range(row_lines):
            at = b * rows_own + t * 128
            ready[at:at + 128, :] = turned(tall[:, t * 128:(t + 1) * 128])
    x = place_x[0]
    found[1], found[2] = jnp.where(first, found[1], found[2]), jnp.where(first, found[2], found[1])
    for index in range(ring):
        value = found[offsets.index(index)]
        for other in range(1, ring):
            value = jnp.where(x == other, found[offsets.index(index ^ other)], value)
        potential[index * row_lines:(index + 1) * row_lines, :] = value


def column_logs(side, xs, cols, logs, stack):
    for q, col in enumerate(cols):
        stack[q] = col[...] if len(col.shape) == 2 else col[side]

    def block(q, worst):
        right = stack[q]
        shift = sampled_shift(xs, right)
        found = shift + jnp.log2(shifted_sum(xs, right, shift, ring * rows_own))
        logs[eight(q), :] = to_lines(found)
        return jnp.maximum(worst, found)

    worst = jnp.full((1, cols_own), -finite_max, jnp.float32)
    worst = lax.fori_loop(0, len(cols), block, worst, unroll=2 if len(cols) > 2 else 1)

    @pl.when(jnp.logical_not(jnp.max(worst) < finite_max))
    def _():
        def exact(q, carry):
            logs[eight(q), :] = to_lines(exact_log([xs], stack[q]))
            return carry

        lax.fori_loop(0, len(cols), exact, 0)


def backward_kernel(flip, core, xs, *refs):
    column_logs(core[0] ^ flip, xs, refs[:-2], refs[-2], refs[-1])


def to_core_kernel(logs, potential, out):
    out[0:32, :] = logs[...]
    out[32:56, :] = potential[...]


def backward_last_kernel(place_z, core, xs, c2, c3, early, swapped, out, logs, stack):
    column_logs(core[0], xs, (c2, c3), logs, stack)
    bits = (0, 1 + 2 * core[0], 3 - 2 * core[0], 2)
    for p, other in enumerate((0, 2, 1, 3)):
        mine = (early if p < 2 else logs)[p % 2 * 8:(p % 2 + 1) * 8, :]
        value = log_add(mine, swapped[other * 8:(other + 1) * 8, :])
        for y in range(ring):
            out[y * ring + (place_z[0] ^ bits[p])] = value


def pack_kernel(core, mine, theirs, out):
    first = core[0] == 0
    for x in range(ring):
        a = mine[32 + x * row_lines:32 + (x + 1) * row_lines, :]
        b = theirs[32 + x * row_lines:32 + (x + 1) * row_lines, :]
        at = 2 * x * row_lines
        out[at:at + row_lines, :] = jnp.where(first, a, b)
        out[at + row_lines:at + 2 * row_lines, :] = jnp.where(first, b, a)


def pack_two_kernel(mine, far, out):
    out[0:48, :] = mine[...]
    out[48:96, :] = far[...]


def final_kernel(place_z, parts, pot, logmass, mine, near, out, potential):
    merged = log_add(*[parts[i] for i in range(ring * ring)])
    out[...] = pot[...] + epsilon * logmass[...] - (epsilon * ln2) * merged
    z = place_z[0]
    for other, ref, at in ((0, mine, 0), (3, mine, 48), (1, near, 0), (2, near, 48)):
        potential[pl.ds(pl.multiple_of((z ^ other) * 48, 8), 48), :] = ref[at:at + 48, :]


def call(kernel, name, out, args, mib=24, pairs=0, scratch=(), scalars=0, last=False):
    within = {} if last else {"out_specs": jax.tree.map(lambda _: pl.BlockSpec(memory_space=pltpu.VMEM), out)}
    specs = [pl.BlockSpec(memory_space=pltpu.SMEM)] * scalars
    specs += [pl.BlockSpec(memory_space=pltpu.VMEM)] * (len(args) - scalars)
    return pl.pallas_call(
        kernel,
        out_shape=out,
        in_specs=specs,
        **within,
        scratch_shapes=list(scratch),
        compiler_params=pltpu.CompilerParams(vmem_limit_bytes=mib << 20),
        cost_estimate=pl.CostEstimate(flops=pairs * 512, bytes_accessed=1 << 20, transcendentals=pairs),
        name=name,
    )(*args)


def across(value, axis, bits):
    return lax.ppermute(value, axis, [(i, i ^ bits) for i in range(ring)])


def across_by_core(value, axis, bits0, bits1):
    pairs = [(2 * i + core, 2 * (i ^ bits) + core) for i in range(ring) for core, bits in enumerate((bits0, bits1))]
    return lax.ppermute(value, (axis, "k"), pairs)


def swap(value):
    return lax.ppermute(value, "k", [(0, 1), (1, 0)])


def after(value, *earlier):
    return lax.optimization_barrier((value, *earlier))[0]


def shape(*dims, dtype=jnp.float32):
    return jax.ShapeDtypeStruct(dims, dtype)


def index_of(axis):
    return lax.axis_index(axis).astype(jnp.int32).reshape(1)


def stack_of(count, *dims):
    return pltpu.VMEM((count, depth, *dims), jnp.bfloat16)


def forward(rows, cols=(), lefts=(), olds=(), mass=()):
    outs = [shape(8 * len(rows) + (8 if mass else 0), 128)]
    n_cols = 2 if cols else 0
    turned_cols = (n_cols * cols_own, 128)
    scratch = [pltpu.VMEM(turned_cols, jnp.bfloat16)] if mass else []
    if cols and not mass:
        outs.append(shape(*turned_cols, dtype=jnp.bfloat16))
    kernel = functools.partial(forward_kernel, len(rows), len(cols), len(lefts), len(olds), len(mass))
    pairs = len(rows) * rows_own * (n_cols + 2 * len(lefts)) * cols_own
    return call(
        kernel, "forward", tuple(outs), (*rows, *cols, *lefts, *olds, *mass), pairs=pairs // 4,
        scratch=scratch + [stack_of(len(rows), rows_own)],
    )


def body(row_points, col_points, row_logmass, col_logmass, col_potential):
    mass_r = row_logmass.reshape(1, rows_own)
    mine = row_points.T
    core = index_of("k")
    bf16 = jnp.bfloat16
    pair = lambda name, mine, theirs: call(
        pair_kernel, name, shape(2, *mine.shape, dtype=bf16), (core, mine, theirs), scalars=1
    )
    pick = lambda name, value: call(
        pick_kernel, name, shape(*value.shape[1:], dtype=bf16), (core, value), scalars=1
    )
    x_pair = pair("pair_rows", mine, swap(mine))
    own = pl.pallas_call(
        prepare_kernel,
        out_shape=shape(depth, cols_own, dtype=jnp.bfloat16),
        in_specs=[pl.BlockSpec(memory_space=pltpu.HBM)] * 3,
        out_specs=pl.BlockSpec(memory_space=pltpu.VMEM),
        scratch_shapes=[
            pltpu.VMEM((dim, cols_own), jnp.bfloat16),
            pltpu.VMEM((1, cols_own), jnp.float32),
            pltpu.VMEM((1, cols_own), jnp.float32),
            pltpu.SemaphoreType.DMA((3,)),
        ],
        compiler_params=pltpu.CompilerParams(vmem_limit_bytes=60 << 20),
        name="prepare",
    )(col_points.T, col_potential.reshape(1, cols_own), col_logmass.reshape(1, cols_own))
    over0 = swap(own)
    x_near = across_by_core(x_pair, "x", 1, 3)
    z_near = across_by_core(pair("pair_cols", own, over0), "z", 1, 3)
    logs, ys0 = forward((mine,), (own, over0))
    x_near = after(x_near, logs)
    x_far = swap(x_near)
    x1 = pick("pick_near", x_near)
    x3 = pick("pick_far", x_far)
    logs2 = forward((x1, x3), lefts=(ys0,))[0]
    z_near = after(z_near, logs2)
    parcel = call(
        parcel_kernel, "parcel", shape(2, depth, cols_own, dtype=bf16), (core, x_near, z_near), scalars=1
    )
    places = [(z, x, c) for z in range(ring) for x in range(ring) for c in range(2)]
    number = {place: i for i, place in enumerate(places)}
    parcel = lax.ppermute(
        parcel, ("z", "x", "k"),
        [(i, number[(z, x ^ 3, 0) if c == 0 else (z ^ 1, x, 1)]) for i, (z, x, c) in enumerate(places)],
    )
    z_far = swap(z_near)
    some = (mine, x1, x3)
    logs, ys1 = forward(some, (z_near,), olds=(logs, logs2))
    z_far = after(z_far, logs)
    logs, ys2 = forward(some, (z_far,), olds=(logs,))
    parcel = after(parcel, logs)
    x2, z2 = call(
        open_kernel, "open", (shape(dim, rows_own, dtype=bf16), shape(2, depth, cols_own, dtype=bf16)),
        (core, parcel, after(swap(parcel), logs)), scalars=1,
    )
    logs2 = forward((x2,), lefts=(ys0, ys1, ys2))[0]
    logs = forward((*some, x2), (z2,), olds=(logs, logs2), mass=(mass_r,))[0]

    fars = [across(logs, "x", d) for d in (1, 3, 2)]
    potential, ready = call(
        merge_rows_kernel, "merge_rows",
        (shape(ring * row_lines, 128), shape(ring * rows_own, 128, dtype=jnp.bfloat16)),
        (index_of("x"), core, logs, *fars, *some, x2), scalars=2,
    )

    block = ring * rows_own * cols_own
    other = call(
        functools.partial(backward_kernel, 1), "backward", shape(32, 128),
        (core, ready, over0, z_near, z_far, z2), pairs=4 * block, scratch=[stack_of(4, cols_own)], scalars=1,
    )
    to_core = call(to_core_kernel, "to_core", shape(56, 128), (other, potential))
    swapped = swap(to_core)
    early = call(
        functools.partial(backward_kernel, 0), "backward", shape(16, 128),
        (core, after(ready, to_core), own, z_near), pairs=2 * block, scratch=[stack_of(2, cols_own)], scalars=1,
    )
    swapped = after(swapped, early)
    chip = call(pack_kernel, "pack", shape(48, 128), (core, to_core, swapped), scalars=1)
    far = across(chip, "z", 3)
    sums = call(
        backward_last_kernel, "backward_last", shape(ring * ring, 8, 128),
        (index_of("z"), core, ready, z_far, z2, early, swapped),
        pairs=2 * block, scratch=[pltpu.VMEM((16, 128), jnp.float32), stack_of(2, cols_own)], scalars=2,
    )
    parts = lax.all_to_all(sums, ("y", "z"), 0, 0)
    chips = call(pack_two_kernel, "pack_two", shape(96, 128), (chip, after(far, sums)))
    new_col, row_potential = call(
        final_kernel, "finish", (shape(8, 128), shape(ring * 48, 128)),
        (index_of("z"), parts, col_potential.reshape(8, 128), col_logmass.reshape(8, 128),
         chips, across(chips, "z", 1)), scalars=1, last=True,
    )
    return row_potential.reshape(-1), new_col.reshape(cols_own)


def solution(mesh):
    fine = Mesh(mesh.devices.reshape(ring, ring, ring, 2), ("y", "z", "x", "k"))
    cols = ("z", "x", "k")
    every = ("y",) + cols
    return jax.shard_map(
        body,
        mesh=fine,
        in_specs=(P(every, None), P(cols, None), P(every), P(cols), P(cols)),
        out_specs=(P("y"), P(cols)),
        check_vma=False,
    )
```

```python
import functools

import jax
import jax.numpy as jnp
from jax import lax
from jax.experimental import pallas as pl
from jax.experimental.pallas import tpu as pltpu
from jax.sharding import Mesh
from jax.sharding import PartitionSpec as P

epsilon = 0.05
dim = 64
rows_own = 768
cols_own = 1024
ring = 4
depth = 80
ln2 = 0.6931471805599453
kappa = 40.0 / ln2
margin = 80.0
chunk = 256
careful = 64
finite_max = 3.0e38
sampled = 64
row_lines = rows_own // 128
offsets = (0, 1, 3, 2)


def split3(v):
    first = v.astype(jnp.bfloat16)
    rest = v - first.astype(jnp.float32)
    second = rest.astype(jnp.bfloat16)
    third = (rest - second.astype(jnp.float32)).astype(jnp.bfloat16)
    return [p.astype(jnp.float32) for p in (first, second, third)]


def place(rows, width):
    index = lax.broadcasted_iota(jnp.int32, (16, width), 0)
    block = jnp.zeros((16, width), jnp.float32)
    for at, row in enumerate(rows):
        block = jnp.where(index == at, jnp.broadcast_to(row, (16, width)), block)
    return block.astype(jnp.bfloat16)


def turned(tile):
    pad = jnp.zeros((128 - depth, 128), jnp.bfloat16)
    return jnp.concatenate([tile, pad], axis=0).T


def score(left, right):
    return lax.dot_general(
        left, right, (((1,), (0,)), ((), ())), preferred_element_type=jnp.float32
    )


def sampled_shift(left, right):
    sample = score(left[0:sampled, 0:depth], right)
    return kappa * jnp.max(sample, axis=0, keepdims=True) + margin


def shifted_sum(left, right, shift, count):
    width = right.shape[1]
    acc = jnp.zeros((8, width), jnp.float32)
    for u in range(count // chunk):
        s = score(left[u * chunk:(u + 1) * chunk, 0:depth], right)
        p = jnp.exp2(s * kappa - shift)
        acc = acc + jnp.sum(p.reshape(chunk // 8, 8, width), axis=0)
    return jnp.sum(acc, axis=0, keepdims=True)


def exact_log(lefts, right):
    width = right.shape[1]
    peak = jnp.full((1, width), -finite_max, jnp.float32)
    total = jnp.zeros((1, width), jnp.float32)

    def rows_at(left, u):
        return left[pl.ds(pl.multiple_of(u * careful, careful), careful), 0:depth]

    for left in lefts:
        def peak_step(u, peak, left=left):
            return jnp.maximum(peak, jnp.max(score(rows_at(left, u), right), axis=0, keepdims=True))

        peak = lax.fori_loop(0, left.shape[0] // careful, peak_step, peak)
    for left in lefts:
        def sum_step(u, total, left=left):
            s = score(rows_at(left, u), right)
            return total + jnp.sum(jnp.exp2((s - peak) * kappa), axis=0, keepdims=True)

        total = lax.fori_loop(0, left.shape[0] // careful, sum_step, total)
    return kappa * peak + jnp.log2(total)


def prepare_kernel(y_far, pot_far, logmass_far, cols_out, y, pot, logmass, done):
    copies = [
        pltpu.make_async_copy(source, target, done.at[i])
        for i, (source, target) in enumerate(((y_far, y), (pot_far, pot), (logmass_far, logmass)))
    ]
    for copy in copies:
        copy.start()
    for copy in copies:
        copy.wait()
    one = jnp.ones((1, cols_own), jnp.float32)
    yw = y[...].astype(jnp.float32)
    norm = jnp.sum(yw * yw, axis=0, keepdims=True)
    c = 0.5 * (pot[...] - norm) + (0.5 * epsilon) * logmass[...]
    cols_out[0:dim, :] = y[...]
    cols_out[dim:depth, :] = place(split3(c) + [one, one, one], cols_own)


def pair_kernel(core, mine, theirs, out):
    out[core[0]] = mine[...]
    out[1 - core[0]] = theirs[...]


def parcel_kernel(core, rows, cols, out):
    @pl.when(core[0] == 0)
    def _():
        out[...] = jnp.zeros(out.shape, jnp.bfloat16)
        out[:, 0:dim, 0:rows_own] = rows[...]

    @pl.when(core[0] == 1)
    def _():
        out[...] = cols[...]


def open_kernel(core, here, there, rows, cols):
    @pl.when(core[0] == 0)
    def _():
        rows[...] = here[0, 0:dim, 0:rows_own]
        cols[...] = there[...]

    @pl.when(core[0] == 1)
    def _():
        rows[...] = there[1, 0:dim, 0:rows_own]
        cols[...] = here[...]


def pick_kernel(core, pair, out):
    out[...] = pair[core[0]]


def to_lines(line):
    count = line.shape[1] // 128
    parts = [line[:, t * 128:(t + 1) * 128] for t in range(count)]
    if count < 8:
        parts.append(jnp.zeros((8 - count, 128), jnp.float32))
    return jnp.concatenate(parts, axis=0)


def eight(at):
    return pl.ds(pl.multiple_of(at * 8, 8), 8)


def log_add(*terms):
    peak = terms[0]
    for t in terms[1:]:
        peak = jnp.maximum(peak, t)
    total = jnp.exp2(terms[0] - peak)
    for t in terms[1:]:
        total = total + jnp.exp2(t - peak)
    return peak + jnp.log2(total)


def line_of(lines, count):
    return jnp.concatenate([lines[t:t + 1, :] for t in range(count)], axis=1)


def forward_kernel(n_rows, n_cols, n_turned, n_old, n_mass, *refs):
    refs = list(refs)
    take = lambda n: [refs.pop(0) for _ in range(n)]
    rows, cols, lefts, olds, mass = take(n_rows), take(n_cols), take(n_turned), take(n_old), take(n_mass)
    if n_cols == 1:
        cols = [cols[0].at[0], cols[0].at[1]]
    out = refs.pop(0)
    stack = refs.pop(-1)
    if cols:
        ys = refs.pop(0)
        for q, col in enumerate(cols):
            def turn(t, carry, q=q, col=col):
                at = pl.multiple_of(t * 128, 128)
                ys[pl.ds(pl.multiple_of(q * cols_own + at, 128), 128), :] = turned(col[:, pl.ds(at, 128)])
                return carry

            lax.fori_loop(0, cols_own // 128, turn, 0, unroll=8)
        lefts = lefts + [ys]
    one = jnp.ones((1, rows_own), jnp.float32)
    extras = place([one, one, one], rows_own)
    for b, row in enumerate(rows):
        stack[b, 0:dim, :] = row[...]
        stack[b, dim:depth, :] = extras
    at = 0
    for old in olds:
        out[at:at + old.shape[0], :] = old[...]
        at += old.shape[0]

    def block(b, worst):
        right = stack[b]
        if olds:
            shift = line_of(out[eight(b), :], row_lines) + margin
            total = 2.0 ** -margin
        else:
            shift = sampled_shift(lefts[0], right)
            total = 0.0
        for left in lefts:
            total = total + shifted_sum(left, right, shift, left.shape[0])
        logs = shift + jnp.log2(total)
        out[eight(b), :] = to_lines(logs)
        return jnp.maximum(worst, logs)

    worst = jnp.full((1, rows_own), -finite_max, jnp.float32)
    worst = lax.fori_loop(0, n_rows, block, worst, unroll={1: 1, 2: 2, 3: 3, 4: 2}[n_rows])

    @pl.when(jnp.logical_not(jnp.max(worst) < finite_max))
    def _():
        at = 0
        for old in olds:
            out[at:at + old.shape[0], :] = old[...]
            at += old.shape[0]

        def exact(b, carry):
            logs = to_lines(exact_log(lefts, stack[b]))
            out[eight(b), :] = log_add(out[eight(b), :], logs) if olds else logs
            return carry

        lax.fori_loop(0, n_rows, exact, 0)

    if mass:
        out[ring * 8:(ring + 1) * 8, :] = to_lines(mass[0][...].astype(jnp.float32))


def merge_rows_kernel(place_x, core, own, far1, far3, far2, x0, x1, x3, x2, potential, ready):
    first = core[0] == 0
    near, far = far1[...], far3[...]
    fars = (own[...], jnp.where(first, near, far), jnp.where(first, far, near), far2[...])
    points = (x0, x1, x3, x2)
    one = jnp.ones((1, rows_own), jnp.float32)
    found = []
    for b in range(ring):
        lines = [(b ^ d) * 8 for d in range(ring)]
        merged = log_add(*[far[n:n + row_lines, :] for n, far in zip(lines, fars)])
        mass = fars[b][ring * 8:ring * 8 + row_lines, :]
        xw = points[b][...].astype(jnp.float32)
        norm = jnp.sum(xw * xw, axis=0, keepdims=True)
        norm = jnp.concatenate([norm[:, t * 128:(t + 1) * 128] for t in range(row_lines)], axis=0)
        found.append(norm - (epsilon * ln2) * merged)
        r = mass * (0.5 * epsilon) - merged * (1.0 / kappa)
        tall = jnp.concatenate(
            [points[b][...], place([one, one, one] + split3(line_of(r, row_lines)), rows_own)], axis=0
        )
        for t in range(row_lines):
            at = b * rows_own + t * 128
            ready[at:at + 128, :] = turned(tall[:, t * 128:(t + 1) * 128])
    x = place_x[0]
    found[1], found[2] = jnp.where(first, found[1], found[2]), jnp.where(first, found[2], found[1])
    for index in range(ring):
        value = found[offsets.index(index)]
        for other in range(1, ring):
            value = jnp.where(x == other, found[offsets.index(index ^ other)], value)
        potential[index * row_lines:(index + 1) * row_lines, :] = value


def column_logs(side, xs, cols, logs, stack):
    for q, col in enumerate(cols):
        stack[q] = col[...] if len(col.shape) == 2 else col[side]

    def block(q, worst):
        right = stack[q]
        shift = sampled_shift(xs, right)
        found = shift + jnp.log2(shifted_sum(xs, right, shift, ring * rows_own))
        logs[eight(q), :] = to_lines(found)
        return jnp.maximum(worst, found)

    worst = jnp.full((1, cols_own), -finite_max, jnp.float32)
    worst = lax.fori_loop(0, len(cols), block, worst, unroll=2)

    @pl.when(jnp.logical_not(jnp.max(worst) < finite_max))
    def _():
        def exact(q, carry):
            logs[eight(q), :] = to_lines(exact_log([xs], stack[q]))
            return carry

        lax.fori_loop(0, len(cols), exact, 0)


def backward_kernel(flip, core, xs, *refs):
    column_logs(core[0] ^ flip, xs, refs[:-2], refs[-2], refs[-1])


def to_core_kernel(logs, potential, out):
    out[0:32, :] = logs[...]
    out[32:56, :] = potential[...]


def backward_last_kernel(place_z, core, xs, c2, c3, early, swapped, out, logs, stack):
    column_logs(core[0], xs, (c2, c3), logs, stack)
    bits = (0, 1 + 2 * core[0], 3 - 2 * core[0], 2)
    for p, other in enumerate((0, 2, 1, 3)):
        mine = (early if p < 2 else logs)[p % 2 * 8:(p % 2 + 1) * 8, :]
        value = log_add(mine, swapped[other * 8:(other + 1) * 8, :])
        for y in range(ring):
            out[y * ring + (place_z[0] ^ bits[p])] = value


def pack_kernel(core, mine, theirs, out):
    first = core[0] == 0
    for x in range(ring):
        a = mine[32 + x * row_lines:32 + (x + 1) * row_lines, :]
        b = theirs[32 + x * row_lines:32 + (x + 1) * row_lines, :]
        at = 2 * x * row_lines
        out[at:at + row_lines, :] = jnp.where(first, a, b)
        out[at + row_lines:at + 2 * row_lines, :] = jnp.where(first, b, a)


def pack_two_kernel(mine, far, out):
    out[0:48, :] = mine[...]
    out[48:96, :] = far[...]


def final_kernel(place_z, parts, pot, logmass, mine, near, out, potential):
    merged = log_add(*[parts[i] for i in range(ring * ring)])
    out[...] = pot[...] + epsilon * logmass[...] - (epsilon * ln2) * merged
    z = place_z[0]
    for other, ref, at in ((0, mine, 0), (3, mine, 48), (1, near, 0), (2, near, 48)):
        potential[pl.ds(pl.multiple_of((z ^ other) * 48, 8), 48), :] = ref[at:at + 48, :]


def call(kernel, name, out, args, mib=24, pairs=0, scratch=(), scalars=0, last=False):
    within = {} if last else {"out_specs": jax.tree.map(lambda _: pl.BlockSpec(memory_space=pltpu.VMEM), out)}
    specs = [pl.BlockSpec(memory_space=pltpu.SMEM)] * scalars
    specs += [pl.BlockSpec(memory_space=pltpu.VMEM)] * (len(args) - scalars)
    return pl.pallas_call(
        kernel,
        out_shape=out,
        in_specs=specs,
        **within,
        scratch_shapes=list(scratch),
        compiler_params=pltpu.CompilerParams(vmem_limit_bytes=mib << 20),
        cost_estimate=pl.CostEstimate(flops=pairs * 512, bytes_accessed=1 << 20, transcendentals=pairs),
        name=name,
    )(*args)


def across(value, axis, bits):
    return lax.ppermute(value, axis, [(i, i ^ bits) for i in range(ring)])


def across_by_core(value, axis, bits0, bits1):
    pairs = [(2 * i + core, 2 * (i ^ bits) + core) for i in range(ring) for core, bits in enumerate((bits0, bits1))]
    return lax.ppermute(value, (axis, "k"), pairs)


def swap(value):
    return lax.ppermute(value, "k", [(0, 1), (1, 0)])


def after(value, *earlier):
    return lax.optimization_barrier((value, *earlier))[0]


def shape(*dims, dtype=jnp.float32):
    return jax.ShapeDtypeStruct(dims, dtype)


def index_of(axis):
    return lax.axis_index(axis).astype(jnp.int32).reshape(1)


def stack_of(count, *dims):
    return pltpu.VMEM((count, depth, *dims), jnp.bfloat16)


def forward(rows, cols=(), lefts=(), olds=(), mass=()):
    outs = [shape(8 * len(rows) + (8 if mass else 0), 128)]
    n_cols = 2 if cols else 0
    turned_cols = (n_cols * cols_own, 128)
    scratch = [pltpu.VMEM(turned_cols, jnp.bfloat16)] if mass else []
    if cols and not mass:
        outs.append(shape(*turned_cols, dtype=jnp.bfloat16))
    kernel = functools.partial(forward_kernel, len(rows), len(cols), len(lefts), len(olds), len(mass))
    pairs = len(rows) * rows_own * (n_cols + 2 * len(lefts)) * cols_own
    return call(
        kernel, "forward", tuple(outs), (*rows, *cols, *lefts, *olds, *mass), pairs=pairs // 4,
        scratch=scratch + [stack_of(len(rows), rows_own)],
    )


def body(row_points, col_points, row_logmass, col_logmass, col_potential):
    mass_r = row_logmass.reshape(1, rows_own)
    mine = row_points.T
    core = index_of("k")
    bf16 = jnp.bfloat16
    pair = lambda name, mine, theirs: call(
        pair_kernel, name, shape(2, *mine.shape, dtype=bf16), (core, mine, theirs), scalars=1
    )
    pick = lambda name, value: call(
        pick_kernel, name, shape(*value.shape[1:], dtype=bf16), (core, value), scalars=1
    )
    x_pair = pair("pair_rows", mine, swap(mine))
    own = pl.pallas_call(
        prepare_kernel,
        out_shape=shape(depth, cols_own, dtype=jnp.bfloat16),
        in_specs=[pl.BlockSpec(memory_space=pltpu.HBM)] * 3,
        out_specs=pl.BlockSpec(memory_space=pltpu.VMEM),
        scratch_shapes=[
            pltpu.VMEM((dim, cols_own), jnp.bfloat16),
            pltpu.VMEM((1, cols_own), jnp.float32),
            pltpu.VMEM((1, cols_own), jnp.float32),
            pltpu.SemaphoreType.DMA((3,)),
        ],
        compiler_params=pltpu.CompilerParams(vmem_limit_bytes=60 << 20),
        name="prepare",
    )(col_points.T, col_potential.reshape(1, cols_own), col_logmass.reshape(1, cols_own))
    over0 = swap(own)
    x_near = across_by_core(x_pair, "x", 1, 3)
    z_near = across_by_core(pair("pair_cols", own, over0), "z", 1, 3)
    logs, ys0 = forward((mine,), (own, over0))
    x_near = after(x_near, logs)
    x_far = swap(x_near)
    x1 = pick("pick_near", x_near)
    x3 = pick("pick_far", x_far)
    logs2 = forward((x1, x3), lefts=(ys0,))[0]
    z_near = after(z_near, logs2)
    parcel = call(
        parcel_kernel, "parcel", shape(2, depth, cols_own, dtype=bf16), (core, x_near, z_near), scalars=1
    )
    places = [(z, x, c) for z in range(ring) for x in range(ring) for c in range(2)]
    number = {place: i for i, place in enumerate(places)}
    parcel = lax.ppermute(
        parcel, ("z", "x", "k"),
        [(i, number[(z, x ^ 3, 0) if c == 0 else (z ^ 1, x, 1)]) for i, (z, x, c) in enumerate(places)],
    )
    z_far = swap(z_near)
    some = (mine, x1, x3)
    logs, ys1 = forward(some, (z_near,), olds=(logs, logs2))
    z_far = after(z_far, logs)
    logs, ys2 = forward(some, (z_far,), olds=(logs,))
    parcel = after(parcel, logs)
    x2, z2 = call(
        open_kernel, "open", (shape(dim, rows_own, dtype=bf16), shape(2, depth, cols_own, dtype=bf16)),
        (core, parcel, after(swap(parcel), logs)), scalars=1,
    )
    logs2 = forward((x2,), lefts=(ys0, ys1, ys2))[0]
    logs = forward((*some, x2), (z2,), olds=(logs, logs2), mass=(mass_r,))[0]

    fars = [across(logs, "x", d) for d in (1, 3, 2)]
    potential, ready = call(
        merge_rows_kernel, "merge_rows",
        (shape(ring * row_lines, 128), shape(ring * rows_own, 128, dtype=jnp.bfloat16)),
        (index_of("x"), core, logs, *fars, *some, x2), scalars=2,
    )

    block = ring * rows_own * cols_own
    other = call(
        functools.partial(backward_kernel, 1), "backward", shape(32, 128),
        (core, ready, over0, z_near, z_far, z2), pairs=4 * block, scratch=[stack_of(4, cols_own)], scalars=1,
    )
    to_core = call(to_core_kernel, "to_core", shape(56, 128), (other, potential))
    swapped = swap(to_core)
    early = call(
        functools.partial(backward_kernel, 0), "backward", shape(16, 128),
        (core, after(ready, to_core), own, z_near), pairs=2 * block, scratch=[stack_of(2, cols_own)], scalars=1,
    )
    swapped = after(swapped, early)
    chip = call(pack_kernel, "pack", shape(48, 128), (core, to_core, swapped), scalars=1)
    far = across(chip, "z", 3)
    sums = call(
        backward_last_kernel, "backward_last", shape(ring * ring, 8, 128),
        (index_of("z"), core, ready, z_far, z2, early, swapped),
        pairs=2 * block, scratch=[pltpu.VMEM((16, 128), jnp.float32), stack_of(2, cols_own)], scalars=2,
    )
    parts = lax.all_to_all(sums, ("y", "z"), 0, 0)
    chips = call(pack_two_kernel, "pack_two", shape(96, 128), (chip, after(far, sums)))
    new_col, row_potential = call(
        final_kernel, "finish", (shape(8, 128), shape(ring * 48, 128)),
        (index_of("z"), parts, col_potential.reshape(8, 128), col_logmass.reshape(8, 128),
         chips, across(chips, "z", 1)), scalars=1, last=True,
    )
    return row_potential.reshape(-1), new_col.reshape(cols_own)


def solution(mesh):
    fine = Mesh(mesh.devices.reshape(ring, ring, ring, 2), ("y", "z", "x", "k"))
    cols = ("z", "x", "k")
    every = ("y",) + cols
    return jax.shard_map(
        body,
        mesh=fine,
        in_specs=(P(every, None), P(cols, None), P(every), P(cols), P(cols)),
        out_specs=(P("y"), P(cols)),
        check_vma=False,
    )
```

```python
import functools

import jax
import jax.numpy as jnp
from jax import lax
from jax.experimental import pallas as pl
from jax.experimental.pallas import tpu as pltpu
from jax.sharding import Mesh
from jax.sharding import PartitionSpec as P

epsilon = 0.05
dim = 64
rows_own = 768
cols_own = 1024
ring = 4
depth = 80
ln2 = 0.6931471805599453
kappa = 40.0 / ln2
margin = 80.0
chunk = 256
careful = 64
finite_max = 3.0e38
sampled = 64
row_lines = rows_own // 128
offsets = (0, 1, 3, 2)


def split3(v):
    first = v.astype(jnp.bfloat16)
    rest = v - first.astype(jnp.float32)
    second = rest.astype(jnp.bfloat16)
    third = (rest - second.astype(jnp.float32)).astype(jnp.bfloat16)
    return [p.astype(jnp.float32) for p in (first, second, third)]


def place(rows, width):
    index = lax.broadcasted_iota(jnp.int32, (16, width), 0)
    block = jnp.zeros((16, width), jnp.float32)
    for at, row in enumerate(rows):
        block = jnp.where(index == at, jnp.broadcast_to(row, (16, width)), block)
    return block.astype(jnp.bfloat16)


def turned(tile):
    pad = jnp.zeros((128 - depth, 128), jnp.bfloat16)
    return jnp.concatenate([tile, pad], axis=0).T


def score(left, right):
    return lax.dot_general(
        left, right, (((1,), (0,)), ((), ())), preferred_element_type=jnp.float32
    )


def sampled_shift(left, right):
    sample = score(left[0:sampled, 0:depth], right)
    return kappa * jnp.max(sample, axis=0, keepdims=True) + margin


def shifted_sum(left, right, shift, count):
    width = right.shape[1]
    acc = jnp.zeros((8, width), jnp.float32)
    for u in range(count // chunk):
        s = score(left[u * chunk:(u + 1) * chunk, 0:depth], right)
        p = jnp.exp2(s * kappa - shift)
        acc = acc + jnp.sum(p.reshape(chunk // 8, 8, width), axis=0)
    return jnp.sum(acc, axis=0, keepdims=True)


def exact_log(lefts, right):
    width = right.shape[1]
    peak = jnp.full((1, width), -finite_max, jnp.float32)
    total = jnp.zeros((1, width), jnp.float32)

    def rows_at(left, u):
        return left[pl.ds(pl.multiple_of(u * careful, careful), careful), 0:depth]

    for left in lefts:
        def peak_step(u, peak, left=left):
            return jnp.maximum(peak, jnp.max(score(rows_at(left, u), right), axis=0, keepdims=True))

        peak = lax.fori_loop(0, left.shape[0] // careful, peak_step, peak)
    for left in lefts:
        def sum_step(u, total, left=left):
            s = score(rows_at(left, u), right)
            return total + jnp.sum(jnp.exp2((s - peak) * kappa), axis=0, keepdims=True)

        total = lax.fori_loop(0, left.shape[0] // careful, sum_step, total)
    return kappa * peak + jnp.log2(total)


def prepare_kernel(y_far, pot_far, logmass_far, cols_out, y, pot, logmass, done):
    copies = [
        pltpu.make_async_copy(source, target, done.at[i])
        for i, (source, target) in enumerate(((y_far, y), (pot_far, pot), (logmass_far, logmass)))
    ]
    for copy in copies:
        copy.start()
    for copy in copies:
        copy.wait()
    one = jnp.ones((1, cols_own), jnp.float32)
    yw = y[...].astype(jnp.float32)
    norm = jnp.sum(yw * yw, axis=0, keepdims=True)
    c = 0.5 * (pot[...] - norm) + (0.5 * epsilon) * logmass[...]
    cols_out[0:dim, :] = y[...]
    cols_out[dim:depth, :] = place(split3(c) + [one, one, one], cols_own)


def pair_kernel(core, mine, theirs, out):
    out[core[0]] = mine[...]
    out[1 - core[0]] = theirs[...]


def parcel_kernel(core, rows, cols, out):
    @pl.when(core[0] == 0)
    def _():
        out[...] = jnp.zeros(out.shape, jnp.bfloat16)
        out[:, 0:dim, 0:rows_own] = rows[...]

    @pl.when(core[0] == 1)
    def _():
        out[...] = cols[...]


def open_kernel(core, here, there, rows, cols):
    @pl.when(core[0] == 0)
    def _():
        rows[...] = here[0, 0:dim, 0:rows_own]
        cols[...] = there[...]

    @pl.when(core[0] == 1)
    def _():
        rows[...] = there[1, 0:dim, 0:rows_own]
        cols[...] = here[...]


def pick_kernel(core, pair, out):
    out[...] = pair[core[0]]


def to_lines(line):
    count = line.shape[1] // 128
    parts = [line[:, t * 128:(t + 1) * 128] for t in range(count)]
    if count < 8:
        parts.append(jnp.zeros((8 - count, 128), jnp.float32))
    return jnp.concatenate(parts, axis=0)


def eight(at):
    return pl.ds(pl.multiple_of(at * 8, 8), 8)


def log_add(*terms):
    peak = terms[0]
    for t in terms[1:]:
        peak = jnp.maximum(peak, t)
    total = jnp.exp2(terms[0] - peak)
    for t in terms[1:]:
        total = total + jnp.exp2(t - peak)
    return peak + jnp.log2(total)


def line_of(lines, count):
    return jnp.concatenate([lines[t:t + 1, :] for t in range(count)], axis=1)


def forward_kernel(n_rows, n_cols, n_turned, n_old, n_mass, *refs):
    refs = list(refs)
    take = lambda n: [refs.pop(0) for _ in range(n)]
    rows, cols, lefts, olds, mass = take(n_rows), take(n_cols), take(n_turned), take(n_old), take(n_mass)
    if n_cols == 1:
        cols = [cols[0].at[0], cols[0].at[1]]
    out = refs.pop(0)
    stack = refs.pop(-1)
    if cols:
        ys = refs.pop(0)
        for q, col in enumerate(cols):
            def turn(t, carry, q=q, col=col):
                at = pl.multiple_of(t * 128, 128)
                ys[pl.ds(pl.multiple_of(q * cols_own + at, 128), 128), :] = turned(col[:, pl.ds(at, 128)])
                return carry

            lax.fori_loop(0, cols_own // 128, turn, 0, unroll=8)
        lefts = lefts + [ys]
    one = jnp.ones((1, rows_own), jnp.float32)
    extras = place([one, one, one], rows_own)
    for b, row in enumerate(rows):
        stack[b, 0:dim, :] = row[...]
        stack[b, dim:depth, :] = extras
    at = 0
    for old in olds:
        out[at:at + old.shape[0], :] = old[...]
        at += old.shape[0]

    def block(b, worst):
        right = stack[b]
        if olds:
            shift = line_of(out[eight(b), :], row_lines) + margin
            total = 2.0 ** -margin
        else:
            shift = sampled_shift(lefts[0], right)
            total = 0.0
        for left in lefts:
            total = total + shifted_sum(left, right, shift, left.shape[0])
        logs = shift + jnp.log2(total)
        out[eight(b), :] = to_lines(logs)
        return jnp.maximum(worst, logs)

    worst = jnp.full((1, rows_own), -finite_max, jnp.float32)
    worst = lax.fori_loop(0, n_rows, block, worst, unroll={1: 1, 2: 2, 3: 3, 4: 2}[n_rows])

    @pl.when(jnp.logical_not(jnp.max(worst) < finite_max))
    def _():
        at = 0
        for old in olds:
            out[at:at + old.shape[0], :] = old[...]
            at += old.shape[0]

        def exact(b, carry):
            logs = to_lines(exact_log(lefts, stack[b]))
            out[eight(b), :] = log_add(out[eight(b), :], logs) if olds else logs
            return carry

        lax.fori_loop(0, n_rows, exact, 0)

    if mass:
        out[ring * 8:(ring + 1) * 8, :] = to_lines(mass[0][...].astype(jnp.float32))


def merge_rows_kernel(place_x, core, own, far1, far3, far2, x0, x1, x3, x2, potential, ready):
    first = core[0] == 0
    near, far = far1[...], far3[...]
    fars = (own[...], jnp.where(first, near, far), jnp.where(first, far, near), far2[...])
    points = (x0, x1, x3, x2)
    one = jnp.ones((1, rows_own), jnp.float32)
    found = []
    for b in range(ring):
        lines = [(b ^ d) * 8 for d in range(ring)]
        merged = log_add(*[far[n:n + row_lines, :] for n, far in zip(lines, fars)])
        mass = fars[b][ring * 8:ring * 8 + row_lines, :]
        xw = points[b][...].astype(jnp.float32)
        norm = jnp.sum(xw * xw, axis=0, keepdims=True)
        norm = jnp.concatenate([norm[:, t * 128:(t + 1) * 128] for t in range(row_lines)], axis=0)
        found.append(norm - (epsilon * ln2) * merged)
        r = mass * (0.5 * epsilon) - merged * (1.0 / kappa)
        tall = jnp.concatenate(
            [points[b][...], place([one, one, one] + split3(line_of(r, row_lines)), rows_own)], axis=0
        )
        for t in range(row_lines):
            at = b * rows_own + t * 128
            ready[at:at + 128, :] = turned(tall[:, t * 128:(t + 1) * 128])
    x = place_x[0]
    found[1], found[2] = jnp.where(first, found[1], found[2]), jnp.where(first, found[2], found[1])
    for index in range(ring):
        value = found[offsets.index(index)]
        for other in range(1, ring):
            value = jnp.where(x == other, found[offsets.index(index ^ other)], value)
        potential[index * row_lines:(index + 1) * row_lines, :] = value


def column_logs(side, xs, cols, logs, stack):
    for q, col in enumerate(cols):
        stack[q] = col[...] if len(col.shape) == 2 else col[side]

    def block(q, worst):
        right = stack[q]
        shift = sampled_shift(xs, right)
        found = shift + jnp.log2(shifted_sum(xs, right, shift, ring * rows_own))
        logs[eight(q), :] = to_lines(found)
        return jnp.maximum(worst, found)

    worst = jnp.full((1, cols_own), -finite_max, jnp.float32)
    worst = lax.fori_loop(0, len(cols), block, worst, unroll=2)

    @pl.when(jnp.logical_not(jnp.max(worst) < finite_max))
    def _():
        def exact(q, carry):
            logs[eight(q), :] = to_lines(exact_log([xs], stack[q]))
            return carry

        lax.fori_loop(0, len(cols), exact, 0)


def backward_kernel(flip, core, xs, *refs):
    column_logs(core[0] ^ flip, xs, refs[:-2], refs[-2], refs[-1])


def to_core_kernel(logs, potential, out):
    out[0:32, :] = logs[...]
    out[32:56, :] = potential[...]


def backward_last_kernel(place_z, core, xs, c2, c3, early, swapped, out, logs, stack):
    column_logs(core[0], xs, (c2, c3), logs, stack)
    bits = (0, 1 + 2 * core[0], 3 - 2 * core[0], 2)
    for p, other in enumerate((0, 2, 1, 3)):
        mine = (early if p < 2 else logs)[p % 2 * 8:(p % 2 + 1) * 8, :]
        value = log_add(mine, swapped[other * 8:(other + 1) * 8, :])
        for y in range(ring):
            out[y * ring + (place_z[0] ^ bits[p])] = value


def pack_kernel(core, mine, theirs, out):
    first = core[0] == 0
    for x in range(ring):
        a = mine[32 + x * row_lines:32 + (x + 1) * row_lines, :]
        b = theirs[32 + x * row_lines:32 + (x + 1) * row_lines, :]
        at = 2 * x * row_lines
        out[at:at + row_lines, :] = jnp.where(first, a, b)
        out[at + row_lines:at + 2 * row_lines, :] = jnp.where(first, b, a)


def pack_two_kernel(mine, far, out):
    out[0:48, :] = mine[...]
    out[48:96, :] = far[...]


def final_kernel(place_z, parts, pot, logmass, mine, near, out, potential):
    merged = log_add(*[parts[i] for i in range(ring * ring)])
    out[...] = pot[...] + epsilon * logmass[...] - (epsilon * ln2) * merged
    z = place_z[0]
    for other, ref, at in ((0, mine, 0), (3, mine, 48), (1, near, 0), (2, near, 48)):
        potential[pl.ds(pl.multiple_of((z ^ other) * 48, 8), 48), :] = ref[at:at + 48, :]


def call(kernel, name, out, args, mib=24, pairs=0, scratch=(), scalars=0, last=False):
    within = {} if last else {"out_specs": jax.tree.map(lambda _: pl.BlockSpec(memory_space=pltpu.VMEM), out)}
    specs = [pl.BlockSpec(memory_space=pltpu.SMEM)] * scalars
    specs += [pl.BlockSpec(memory_space=pltpu.VMEM)] * (len(args) - scalars)
    return pl.pallas_call(
        kernel,
        out_shape=out,
        in_specs=specs,
        **within,
        scratch_shapes=list(scratch),
        compiler_params=pltpu.CompilerParams(vmem_limit_bytes=mib << 20),
        cost_estimate=pl.CostEstimate(flops=pairs * 512, bytes_accessed=1 << 20, transcendentals=pairs),
        name=name,
    )(*args)


def across(value, axis, bits):
    return lax.ppermute(value, axis, [(i, i ^ bits) for i in range(ring)])


def across_by_core(value, axis, bits0, bits1):
    pairs = [(2 * i + core, 2 * (i ^ bits) + core) for i in range(ring) for core, bits in enumerate((bits0, bits1))]
    return lax.ppermute(value, (axis, "k"), pairs)


def swap(value):
    return lax.ppermute(value, "k", [(0, 1), (1, 0)])


def after(value, *earlier):
    return lax.optimization_barrier((value, *earlier))[0]


def shape(*dims, dtype=jnp.float32):
    return jax.ShapeDtypeStruct(dims, dtype)


def index_of(axis):
    return lax.axis_index(axis).astype(jnp.int32).reshape(1)


def stack_of(count, *dims):
    return pltpu.VMEM((count, depth, *dims), jnp.bfloat16)


def forward(rows, cols=(), lefts=(), olds=(), mass=()):
    outs = [shape(8 * len(rows) + (8 if mass else 0), 128)]
    n_cols = 2 if cols else 0
    turned_cols = (n_cols * cols_own, 128)
    scratch = [pltpu.VMEM(turned_cols, jnp.bfloat16)] if mass else []
    if cols and not mass:
        outs.append(shape(*turned_cols, dtype=jnp.bfloat16))
    kernel = functools.partial(forward_kernel, len(rows), len(cols), len(lefts), len(olds), len(mass))
    pairs = len(rows) * rows_own * (n_cols + 2 * len(lefts)) * cols_own
    return call(
        kernel, "forward", tuple(outs), (*rows, *cols, *lefts, *olds, *mass), pairs=pairs // 4,
        scratch=scratch + [stack_of(len(rows), rows_own)],
    )


def body(row_points, col_points, row_logmass, col_logmass, col_potential):
    mass_r = row_logmass.reshape(1, rows_own)
    mine = row_points.T
    core = index_of("k")
    bf16 = jnp.bfloat16
    pair = lambda name, mine, theirs: call(
        pair_kernel, name, shape(2, *mine.shape, dtype=bf16), (core, mine, theirs), scalars=1
    )
    pick = lambda name, value: call(
        pick_kernel, name, shape(*value.shape[1:], dtype=bf16), (core, value), scalars=1
    )
    x_pair = pair("pair_rows", mine, swap(mine))
    own = pl.pallas_call(
        prepare_kernel,
        out_shape=shape(depth, cols_own, dtype=jnp.bfloat16),
        in_specs=[pl.BlockSpec(memory_space=pltpu.HBM)] * 3,
        out_specs=pl.BlockSpec(memory_space=pltpu.VMEM),
        scratch_shapes=[
            pltpu.VMEM((dim, cols_own), jnp.bfloat16),
            pltpu.VMEM((1, cols_own), jnp.float32),
            pltpu.VMEM((1, cols_own), jnp.float32),
            pltpu.SemaphoreType.DMA((3,)),
        ],
        compiler_params=pltpu.CompilerParams(vmem_limit_bytes=60 << 20),
        name="prepare",
    )(col_points.T, col_potential.reshape(1, cols_own), col_logmass.reshape(1, cols_own))
    over0 = swap(own)
    x_near = across_by_core(x_pair, "x", 1, 3)
    z_near = across_by_core(pair("pair_cols", own, over0), "z", 1, 3)
    logs, ys0 = forward((mine,), (own, over0))
    x_near = after(x_near, logs)
    x_far = swap(x_near)
    x1 = pick("pick_near", x_near)
    logs1 = forward((x1,), lefts=(ys0,))[0]
    x_far = after(x_far, logs1)
    x3 = pick("pick_far", x_far)
    logs2 = forward((x3,), lefts=(ys0,))[0]
    z_near = after(z_near, logs2)
    parcel = call(
        parcel_kernel, "parcel", shape(2, depth, cols_own, dtype=bf16), (core, x_near, z_near), scalars=1
    )
    places = [(z, x, c) for z in range(ring) for x in range(ring) for c in range(2)]
    number = {place: i for i, place in enumerate(places)}
    parcel = lax.ppermute(
        parcel, ("z", "x", "k"),
        [(i, number[(z, x ^ 3, 0) if c == 0 else (z ^ 1, x, 1)]) for i, (z, x, c) in enumerate(places)],
    )
    z_far = swap(z_near)
    some = (mine, x1, x3)
    logs, ys1 = forward(some, (z_near,), olds=(logs, logs1, logs2))
    z_far = after(z_far, logs)
    logs, ys2 = forward(some, (z_far,), olds=(logs,))
    parcel = after(parcel, logs)
    x2, z2 = call(
        open_kernel, "open", (shape(dim, rows_own, dtype=bf16), shape(2, depth, cols_own, dtype=bf16)),
        (core, parcel, after(swap(parcel), logs)), scalars=1,
    )
    logs2 = forward((x2,), lefts=(ys0, ys1, ys2))[0]
    logs = forward((*some, x2), (z2,), olds=(logs, logs2), mass=(mass_r,))[0]

    fars = [across(logs, "x", d) for d in (1, 3, 2)]
    potential, ready = call(
        merge_rows_kernel, "merge_rows",
        (shape(ring * row_lines, 128), shape(ring * rows_own, 128, dtype=jnp.bfloat16)),
        (index_of("x"), core, logs, *fars, *some, x2), scalars=2,
    )

    block = ring * rows_own * cols_own
    other = call(
        functools.partial(backward_kernel, 1), "backward", shape(32, 128),
        (core, ready, over0, z_near, z_far, z2), pairs=4 * block, scratch=[stack_of(4, cols_own)], scalars=1,
    )
    to_core = call(to_core_kernel, "to_core", shape(56, 128), (other, potential))
    swapped = swap(to_core)
    early = call(
        functools.partial(backward_kernel, 0), "backward", shape(16, 128),
        (core, after(ready, to_core), own, z_near), pairs=2 * block, scratch=[stack_of(2, cols_own)], scalars=1,
    )
    swapped = after(swapped, early)
    chip = call(pack_kernel, "pack", shape(48, 128), (core, to_core, swapped), scalars=1)
    far = across(chip, "z", 3)
    sums = call(
        backward_last_kernel, "backward_last", shape(ring * ring, 8, 128),
        (index_of("z"), core, ready, z_far, z2, early, swapped),
        pairs=2 * block, scratch=[pltpu.VMEM((16, 128), jnp.float32), stack_of(2, cols_own)], scalars=2,
    )
    parts = lax.all_to_all(sums, ("y", "z"), 0, 0)
    chips = call(pack_two_kernel, "pack_two", shape(96, 128), (chip, after(far, sums)))
    new_col, row_potential = call(
        final_kernel, "finish", (shape(8, 128), shape(ring * 48, 128)),
        (index_of("z"), parts, col_potential.reshape(8, 128), col_logmass.reshape(8, 128),
         chips, across(chips, "z", 1)), scalars=1, last=True,
    )
    return row_potential.reshape(-1), new_col.reshape(cols_own)


def solution(mesh):
    fine = Mesh(mesh.devices.reshape(ring, ring, ring, 2), ("y", "z", "x", "k"))
    cols = ("z", "x", "k")
    every = ("y",) + cols
    return jax.shard_map(
        body,
        mesh=fine,
        in_specs=(P(every, None), P(cols, None), P(every), P(cols), P(cols)),
        out_specs=(P("y"), P(cols)),
        check_vma=False,
    )
```

```python
import functools

import jax
import jax.numpy as jnp
from jax import lax
from jax.experimental import pallas as pl
from jax.experimental.pallas import tpu as pltpu
from jax.sharding import Mesh
from jax.sharding import PartitionSpec as P

epsilon = 0.05
dim = 64
rows_own = 768
cols_own = 1024
ring = 4
depth = 80
ln2 = 0.6931471805599453
kappa = 40.0 / ln2
margin = 80.0
chunk = 256
careful = 64
finite_max = 3.0e38
sampled = 64
row_lines = rows_own // 128
offsets = (0, 1, 3, 2)


def split3(v):
    first = v.astype(jnp.bfloat16)
    rest = v - first.astype(jnp.float32)
    second = rest.astype(jnp.bfloat16)
    third = (rest - second.astype(jnp.float32)).astype(jnp.bfloat16)
    return [p.astype(jnp.float32) for p in (first, second, third)]


def place(rows, width):
    index = lax.broadcasted_iota(jnp.int32, (16, width), 0)
    block = jnp.zeros((16, width), jnp.float32)
    for at, row in enumerate(rows):
        block = jnp.where(index == at, jnp.broadcast_to(row, (16, width)), block)
    return block.astype(jnp.bfloat16)


def turned(tile):
    pad = jnp.zeros((128 - depth, 128), jnp.bfloat16)
    return jnp.concatenate([tile, pad], axis=0).T


def score(left, right):
    return lax.dot_general(
        left, right, (((1,), (0,)), ((), ())), preferred_element_type=jnp.float32
    )


def sampled_shift(left, right):
    sample = score(left[0:sampled, 0:depth], right)
    return kappa * jnp.max(sample, axis=0, keepdims=True) + margin


def shifted_sum(left, right, shift, count):
    width = right.shape[1]
    acc = jnp.zeros((8, width), jnp.float32)
    for u in range(count // chunk):
        s = score(left[u * chunk:(u + 1) * chunk, 0:depth], right)
        p = jnp.exp2(s * kappa - shift)
        acc = acc + jnp.sum(p.reshape(chunk // 8, 8, width), axis=0)
    return jnp.sum(acc, axis=0, keepdims=True)


def exact_log(lefts, right):
    width = right.shape[1]
    peak = jnp.full((1, width), -finite_max, jnp.float32)
    total = jnp.zeros((1, width), jnp.float32)

    def rows_at(left, u):
        return left[pl.ds(pl.multiple_of(u * careful, careful), careful), 0:depth]

    for left in lefts:
        def peak_step(u, peak, left=left):
            return jnp.maximum(peak, jnp.max(score(rows_at(left, u), right), axis=0, keepdims=True))

        peak = lax.fori_loop(0, left.shape[0] // careful, peak_step, peak)
    for left in lefts:
        def sum_step(u, total, left=left):
            s = score(rows_at(left, u), right)
            return total + jnp.sum(jnp.exp2((s - peak) * kappa), axis=0, keepdims=True)

        total = lax.fori_loop(0, left.shape[0] // careful, sum_step, total)
    return kappa * peak + jnp.log2(total)


def prepare_kernel(y_far, pot_far, logmass_far, cols_out, y, pot, logmass, done):
    copies = [
        pltpu.make_async_copy(source, target, done.at[i])
        for i, (source, target) in enumerate(((y_far, y), (pot_far, pot), (logmass_far, logmass)))
    ]
    for copy in copies:
        copy.start()
    for copy in copies:
        copy.wait()
    one = jnp.ones((1, cols_own), jnp.float32)
    yw = y[...].astype(jnp.float32)
    norm = jnp.sum(yw * yw, axis=0, keepdims=True)
    c = 0.5 * (pot[...] - norm) + (0.5 * epsilon) * logmass[...]
    cols_out[0:dim, :] = y[...]
    cols_out[dim:depth, :] = place(split3(c) + [one, one, one], cols_own)


def pair_kernel(core, mine, theirs, out):
    out[core[0]] = mine[...]
    out[1 - core[0]] = theirs[...]


def parcel_kernel(core, rows, cols, out):
    @pl.when(core[0] == 0)
    def _():
        out[...] = jnp.zeros(out.shape, jnp.bfloat16)
        out[:, 0:dim, 0:rows_own] = rows[...]

    @pl.when(core[0] == 1)
    def _():
        out[...] = cols[...]


def open_kernel(core, here, there, rows, cols):
    @pl.when(core[0] == 0)
    def _():
        rows[...] = here[0, 0:dim, 0:rows_own]
        cols[...] = there[...]

    @pl.when(core[0] == 1)
    def _():
        rows[...] = there[1, 0:dim, 0:rows_own]
        cols[...] = here[...]


def pick_kernel(core, pair, out):
    out[...] = pair[core[0]]


def to_lines(line):
    count = line.shape[1] // 128
    parts = [line[:, t * 128:(t + 1) * 128] for t in range(count)]
    if count < 8:
        parts.append(jnp.zeros((8 - count, 128), jnp.float32))
    return jnp.concatenate(parts, axis=0)


def eight(at):
    return pl.ds(pl.multiple_of(at * 8, 8), 8)


def log_add(*terms):
    peak = terms[0]
    for t in terms[1:]:
        peak = jnp.maximum(peak, t)
    total = jnp.exp2(terms[0] - peak)
    for t in terms[1:]:
        total = total + jnp.exp2(t - peak)
    return peak + jnp.log2(total)


def line_of(lines, count):
    return jnp.concatenate([lines[t:t + 1, :] for t in range(count)], axis=1)


def forward_kernel(n_rows, n_cols, n_turned, n_old, n_mass, *refs):
    refs = list(refs)
    take = lambda n: [refs.pop(0) for _ in range(n)]
    rows, cols, lefts, olds, mass = take(n_rows), take(n_cols), take(n_turned), take(n_old), take(n_mass)
    if n_cols == 1:
        cols = [cols[0].at[0], cols[0].at[1]]
    out = refs.pop(0)
    stack = refs.pop(-1)
    if cols:
        ys = refs.pop(0)
        for q, col in enumerate(cols):
            def turn(t, carry, q=q, col=col):
                at = pl.multiple_of(t * 128, 128)
                ys[pl.ds(pl.multiple_of(q * cols_own + at, 128), 128), :] = turned(col[:, pl.ds(at, 128)])
                return carry

            lax.fori_loop(0, cols_own // 128, turn, 0, unroll=8)
        lefts = lefts + [ys]
    one = jnp.ones((1, rows_own), jnp.float32)
    extras = place([one, one, one], rows_own)
    for b, row in enumerate(rows):
        stack[b, 0:dim, :] = row[...]
        stack[b, dim:depth, :] = extras
    at = 0
    for old in olds:
        out[at:at + old.shape[0], :] = old[...]
        at += old.shape[0]

    def block(b, worst):
        right = stack[b]
        if olds:
            shift = line_of(out[eight(b), :], row_lines) + margin
            total = 2.0 ** -margin
        else:
            shift = sampled_shift(lefts[0], right)
            total = 0.0
        for left in lefts:
            total = total + shifted_sum(left, right, shift, left.shape[0])
        logs = shift + jnp.log2(total)
        out[eight(b), :] = to_lines(logs)
        return jnp.maximum(worst, logs)

    worst = jnp.full((1, rows_own), -finite_max, jnp.float32)
    worst = lax.fori_loop(0, n_rows, block, worst, unroll=n_rows)

    @pl.when(jnp.logical_not(jnp.max(worst) < finite_max))
    def _():
        at = 0
        for old in olds:
            out[at:at + old.shape[0], :] = old[...]
            at += old.shape[0]

        def exact(b, carry):
            logs = to_lines(exact_log(lefts, stack[b]))
            out[eight(b), :] = log_add(out[eight(b), :], logs) if olds else logs
            return carry

        lax.fori_loop(0, n_rows, exact, 0)

    if mass:
        out[ring * 8:(ring + 1) * 8, :] = to_lines(mass[0][...].astype(jnp.float32))


def merge_rows_kernel(place_x, core, own, far1, far3, far2, x0, x1, x3, x2, potential, ready):
    first = core[0] == 0
    near, far = far1[...], far3[...]
    fars = (own[...], jnp.where(first, near, far), jnp.where(first, far, near), far2[...])
    points = (x0, x1, x3, x2)
    one = jnp.ones((1, rows_own), jnp.float32)
    found = []
    for b in range(ring):
        lines = [(b ^ d) * 8 for d in range(ring)]
        merged = log_add(*[far[n:n + row_lines, :] for n, far in zip(lines, fars)])
        mass = fars[b][ring * 8:ring * 8 + row_lines, :]
        xw = points[b][...].astype(jnp.float32)
        norm = jnp.sum(xw * xw, axis=0, keepdims=True)
        norm = jnp.concatenate([norm[:, t * 128:(t + 1) * 128] for t in range(row_lines)], axis=0)
        found.append(norm - (epsilon * ln2) * merged)
        r = mass * (0.5 * epsilon) - merged * (1.0 / kappa)
        tall = jnp.concatenate(
            [points[b][...], place([one, one, one] + split3(line_of(r, row_lines)), rows_own)], axis=0
        )
        for t in range(row_lines):
            at = b * rows_own + t * 128
            ready[at:at + 128, :] = turned(tall[:, t * 128:(t + 1) * 128])
    x = place_x[0]
    found[1], found[2] = jnp.where(first, found[1], found[2]), jnp.where(first, found[2], found[1])
    for index in range(ring):
        value = found[offsets.index(index)]
        for other in range(1, ring):
            value = jnp.where(x == other, found[offsets.index(index ^ other)], value)
        potential[index * row_lines:(index + 1) * row_lines, :] = value


def column_logs(side, xs, cols, logs, stack):
    for q, col in enumerate(cols):
        stack[q] = col[...] if len(col.shape) == 2 else col[side]

    def block(q, worst):
        right = stack[q]
        shift = sampled_shift(xs, right)
        found = shift + jnp.log2(shifted_sum(xs, right, shift, ring * rows_own))
        logs[eight(q), :] = to_lines(found)
        return jnp.maximum(worst, found)

    worst = jnp.full((1, cols_own), -finite_max, jnp.float32)
    worst = lax.fori_loop(0, len(cols), block, worst, unroll=len(cols))

    @pl.when(jnp.logical_not(jnp.max(worst) < finite_max))
    def _():
        def exact(q, carry):
            logs[eight(q), :] = to_lines(exact_log([xs], stack[q]))
            return carry

        lax.fori_loop(0, len(cols), exact, 0)


def backward_kernel(flip, core, xs, *refs):
    column_logs(core[0] ^ flip, xs, refs[:-2], refs[-2], refs[-1])


def to_core_kernel(logs, potential, out):
    out[0:32, :] = logs[...]
    out[32:56, :] = potential[...]


def backward_last_kernel(place_z, core, xs, c2, c3, early, swapped, out, logs, stack):
    column_logs(core[0], xs, (c2, c3), logs, stack)
    bits = (0, 1 + 2 * core[0], 3 - 2 * core[0], 2)
    for p, other in enumerate((0, 2, 1, 3)):
        mine = (early if p < 2 else logs)[p % 2 * 8:(p % 2 + 1) * 8, :]
        value = log_add(mine, swapped[other * 8:(other + 1) * 8, :])
        for y in range(ring):
            out[y * ring + (place_z[0] ^ bits[p])] = value


def pack_kernel(core, mine, theirs, out):
    first = core[0] == 0
    for x in range(ring):
        a = mine[32 + x * row_lines:32 + (x + 1) * row_lines, :]
        b = theirs[32 + x * row_lines:32 + (x + 1) * row_lines, :]
        at = 2 * x * row_lines
        out[at:at + row_lines, :] = jnp.where(first, a, b)
        out[at + row_lines:at + 2 * row_lines, :] = jnp.where(first, b, a)


def pack_two_kernel(mine, far, out):
    out[0:48, :] = mine[...]
    out[48:96, :] = far[...]


def final_kernel(place_z, parts, pot, logmass, mine, near, out, potential):
    merged = log_add(*[parts[i] for i in range(ring * ring)])
    out[...] = pot[...] + epsilon * logmass[...] - (epsilon * ln2) * merged
    z = place_z[0]
    for other, ref, at in ((0, mine, 0), (3, mine, 48), (1, near, 0), (2, near, 48)):
        potential[pl.ds(pl.multiple_of((z ^ other) * 48, 8), 48), :] = ref[at:at + 48, :]


def call(kernel, name, out, args, mib=24, pairs=0, scratch=(), scalars=0, last=False):
    within = {} if last else {"out_specs": jax.tree.map(lambda _: pl.BlockSpec(memory_space=pltpu.VMEM), out)}
    specs = [pl.BlockSpec(memory_space=pltpu.SMEM)] * scalars
    specs += [pl.BlockSpec(memory_space=pltpu.VMEM)] * (len(args) - scalars)
    return pl.pallas_call(
        kernel,
        out_shape=out,
        in_specs=specs,
        **within,
        scratch_shapes=list(scratch),
        compiler_params=pltpu.CompilerParams(vmem_limit_bytes=mib << 20),
        cost_estimate=pl.CostEstimate(flops=pairs * 512, bytes_accessed=1 << 20, transcendentals=pairs),
        name=name,
    )(*args)


def across(value, axis, bits):
    return lax.ppermute(value, axis, [(i, i ^ bits) for i in range(ring)])


def across_by_core(value, axis, bits0, bits1):
    pairs = [(2 * i + core, 2 * (i ^ bits) + core) for i in range(ring) for core, bits in enumerate((bits0, bits1))]
    return lax.ppermute(value, (axis, "k"), pairs)


def swap(value):
    return lax.ppermute(value, "k", [(0, 1), (1, 0)])


def after(value, *earlier):
    return lax.optimization_barrier((value, *earlier))[0]


def shape(*dims, dtype=jnp.float32):
    return jax.ShapeDtypeStruct(dims, dtype)


def index_of(axis):
    return lax.axis_index(axis).astype(jnp.int32).reshape(1)


def stack_of(count, *dims):
    return pltpu.VMEM((count, depth, *dims), jnp.bfloat16)


def forward(rows, cols=(), lefts=(), olds=(), mass=()):
    outs = [shape(8 * len(rows) + (8 if mass else 0), 128)]
    n_cols = 2 if cols else 0
    turned_cols = (n_cols * cols_own, 128)
    scratch = [pltpu.VMEM(turned_cols, jnp.bfloat16)] if mass else []
    if cols and not mass:
        outs.append(shape(*turned_cols, dtype=jnp.bfloat16))
    kernel = functools.partial(forward_kernel, len(rows), len(cols), len(lefts), len(olds), len(mass))
    pairs = len(rows) * rows_own * (n_cols + 2 * len(lefts)) * cols_own
    return call(
        kernel, "forward", tuple(outs), (*rows, *cols, *lefts, *olds, *mass), pairs=pairs // 4,
        scratch=scratch + [stack_of(len(rows), rows_own)],
    )


def body(row_points, col_points, row_logmass, col_logmass, col_potential):
    mass_r = row_logmass.reshape(1, rows_own)
    mine = row_points.T
    core = index_of("k")
    bf16 = jnp.bfloat16
    pair = lambda name, mine, theirs: call(
        pair_kernel, name, shape(2, *mine.shape, dtype=bf16), (core, mine, theirs), scalars=1
    )
    pick = lambda name, value: call(
        pick_kernel, name, shape(*value.shape[1:], dtype=bf16), (core, value), scalars=1
    )
    x_pair = pair("pair_rows", mine, swap(mine))
    own = pl.pallas_call(
        prepare_kernel,
        out_shape=shape(depth, cols_own, dtype=jnp.bfloat16),
        in_specs=[pl.BlockSpec(memory_space=pltpu.HBM)] * 3,
        out_specs=pl.BlockSpec(memory_space=pltpu.VMEM),
        scratch_shapes=[
            pltpu.VMEM((dim, cols_own), jnp.bfloat16),
            pltpu.VMEM((1, cols_own), jnp.float32),
            pltpu.VMEM((1, cols_own), jnp.float32),
            pltpu.SemaphoreType.DMA((3,)),
        ],
        compiler_params=pltpu.CompilerParams(vmem_limit_bytes=60 << 20),
        name="prepare",
    )(col_points.T, col_potential.reshape(1, cols_own), col_logmass.reshape(1, cols_own))
    over0 = swap(own)
    x_near = across_by_core(x_pair, "x", 1, 3)
    z_near = across_by_core(pair("pair_cols", own, over0), "z", 1, 3)
    logs, ys0 = forward((mine,), (own, over0))
    x_near = after(x_near, logs)
    x_far = swap(x_near)
    x1 = pick("pick_near", x_near)
    logs1 = forward((x1,), lefts=(ys0,))[0]
    x_far = after(x_far, logs1)
    x3 = pick("pick_far", x_far)
    logs2 = forward((x3,), lefts=(ys0,))[0]
    z_near = after(z_near, logs2)
    parcel = call(
        parcel_kernel, "parcel", shape(2, depth, cols_own, dtype=bf16), (core, x_near, z_near), scalars=1
    )
    places = [(z, x, c) for z in range(ring) for x in range(ring) for c in range(2)]
    number = {place: i for i, place in enumerate(places)}
    parcel = lax.ppermute(
        parcel, ("z", "x", "k"),
        [(i, number[(z, x ^ 3, 0) if c == 0 else (z ^ 1, x, 1)]) for i, (z, x, c) in enumerate(places)],
    )
    z_far = swap(z_near)
    some = (mine, x1, x3)
    logs, ys1 = forward(some, (z_near,), olds=(logs, logs1, logs2))
    z_far = after(z_far, logs)
    logs, ys2 = forward(some, (z_far,), olds=(logs,))
    parcel = after(parcel, logs)
    x2, z2 = call(
        open_kernel, "open", (shape(dim, rows_own, dtype=bf16), shape(2, depth, cols_own, dtype=bf16)),
        (core, parcel, after(swap(parcel), logs)), scalars=1,
    )
    logs2 = forward((x2,), lefts=(ys0, ys1, ys2))[0]
    logs = forward((*some, x2), (z2,), olds=(logs, logs2), mass=(mass_r,))[0]

    fars = [across(logs, "x", d) for d in (1, 3, 2)]
    potential, ready = call(
        merge_rows_kernel, "merge_rows",
        (shape(ring * row_lines, 128), shape(ring * rows_own, 128, dtype=jnp.bfloat16)),
        (index_of("x"), core, logs, *fars, *some, x2), scalars=2,
    )

    block = ring * rows_own * cols_own
    other = call(
        functools.partial(backward_kernel, 1), "backward", shape(32, 128),
        (core, ready, over0, z_near, z_far, z2), pairs=4 * block, scratch=[stack_of(4, cols_own)], scalars=1,
    )
    to_core = call(to_core_kernel, "to_core", shape(56, 128), (other, potential))
    swapped = swap(to_core)
    early = call(
        functools.partial(backward_kernel, 0), "backward", shape(16, 128),
        (core, after(ready, to_core), own, z_near), pairs=2 * block, scratch=[stack_of(2, cols_own)], scalars=1,
    )
    swapped = after(swapped, early)
    chip = call(pack_kernel, "pack", shape(48, 128), (core, to_core, swapped), scalars=1)
    far = across(chip, "z", 3)
    sums = call(
        backward_last_kernel, "backward_last", shape(ring * ring, 8, 128),
        (index_of("z"), core, ready, z_far, z2, early, swapped),
        pairs=2 * block, scratch=[pltpu.VMEM((16, 128), jnp.float32), stack_of(2, cols_own)], scalars=2,
    )
    parts = lax.all_to_all(sums, ("y", "z"), 0, 0)
    chips = call(pack_two_kernel, "pack_two", shape(96, 128), (chip, after(far, sums)))
    new_col, row_potential = call(
        final_kernel, "finish", (shape(8, 128), shape(ring * 48, 128)),
        (index_of("z"), parts, col_potential.reshape(8, 128), col_logmass.reshape(8, 128),
         chips, across(chips, "z", 1)), scalars=1, last=True,
    )
    return row_potential.reshape(-1), new_col.reshape(cols_own)


def solution(mesh):
    fine = Mesh(mesh.devices.reshape(ring, ring, ring, 2), ("y", "z", "x", "k"))
    cols = ("z", "x", "k")
    every = ("y",) + cols
    return jax.shard_map(
        body,
        mesh=fine,
        in_specs=(P(every, None), P(cols, None), P(every), P(cols), P(cols)),
        out_specs=(P("y"), P(cols)),
        check_vma=False,
    )
```
